256 devices in a mesh: pair: 32 (over x, z), mom: 8 (over y, core).
Axes of the slice: x: 4, y: 4, z: 8, core: 2. Of those that a mesh axis runs over, the one named last changes fastest.
Arguments:
- peramb: bfloat16 [32, 768, 1536], P(None, 'pair'), may hold values from -0.21875 to 0.21875
- elementals: bfloat16 [16, 8, 2, 192, 384], P(None, 'mom'), may hold values from -0.4375 to 0.4375
- pair_times: int32 [32, 2], replicated, may hold values from 0 to 15
- pair_order: int32 [32], replicated, may hold values from 0 to 31, each once
- class_group: int32 [8], P('mom'), may hold values from 0 to 7
- gamma_columns: int32 [2, 4], replicated, may hold values from 0 to 3, each once within a row
- gamma_phases: int32 [2, 4], replicated, may hold values from 0 to 3
Outputs:
- correlator: float32 [2, 32, 8], P(None, 'pair')
The draws below stay inside these ranges and needn't reach their ends.
Inputs may be any that keep to these rules, and one draw needn't show every extreme that they name: `pair_order`: each pair stands in exactly one slot. `gamma_columns`: each row is a permutation of the 4 spins.
All inputs are finite; a program needn't handle non-finite values.
Results may differ from the reference program's by a relative error of at most 0.0063.
Values may be sent and summed in bfloat16 or wider, within the bound.
A program may use at most 128 MiB of HBM per device.

```python
import jax
import jax.numpy as jnp
from jax import lax

NS = 4
NEV = 192
NT = 16
GROUPS = 8
NPAIRS = 32
CLASSES = 8


def plant(result, rng, low, largest):
    index_at = [jax.random.randint(jax.random.fold_in(rng, axis), (), 0, length) for axis, length in enumerate(result.shape)]
    main_axis = result.shape.index(max(result.shape))
    next_to = index_at[:main_axis] + [(index_at[main_axis] + 1) % result.shape[main_axis]] + index_at[main_axis + 1:]
    return result.at[tuple(index_at)].set(low).at[tuple(next_to)].set(largest)


def block_scale(own_key, shape, split, smallest, high):
    gain = 1.0
    for dim, shards_of in split:
        heights = jax.random.uniform(jax.random.fold_in(jax.random.fold_in(own_key, 6), dim), (shards_of,), jnp.float32, smallest / len(split), high / len(split))
        gain = gain * jnp.repeat(jnp.exp(heights), shape[dim] // shards_of).reshape((-1,) + (1,) * (len(shape) - 1 - dim))
    return gain


def noise(rng, shape, width, bound, split=(), held_as=jnp.bfloat16):
    array = jax.random.normal(rng, shape, jnp.float32) * width
    if len(split) > 0:
        array = block_scale(rng, shape, split, -0.22, 0.18) * array
    return jnp.clip(array, min=-bound, max=bound).astype(held_as)


def setup_inputs(seed: int = 0) -> dict:
    keys = jax.random.split(jax.random.key(seed), 8)
    return {
        "peramb": noise(keys[0], (NPAIRS, NS * NEV, 2 * NS * NEV), (NS * NEV) ** -0.5, 0.21875, ((1, 32),)),
        "elementals": noise(keys[1], (NT, CLASSES, 2, NEV, 2 * NEV), NEV ** -0.5, 0.4375, ((1, 8),)),
        "pair_times": plant(jax.random.randint(keys[2], (NPAIRS, 2), 0, NT), jax.random.fold_in(keys[2], 1), 0, NT - 1).astype(jnp.int32),
        "pair_order": jax.random.permutation(keys[3], NPAIRS).astype(jnp.int32),
        "class_group": plant(jax.random.randint(keys[4], (CLASSES,), 0, GROUPS), jax.random.fold_in(keys[4], 1), 0, GROUPS - 1).astype(jnp.int32),
        "gamma_columns": jax.vmap(lambda own: jax.random.permutation(own, NS))(jax.random.split(keys[5], 2)).reshape((2, NS)).astype(jnp.int32),
        "gamma_phases": plant(jax.random.randint(keys[6], (2, NS), 0, 4), jax.random.fold_in(keys[6], 1), 0, 3).astype(jnp.int32),
    }


def gamma_matrix(columns, phases):
    spin_index = jnp.arange(columns.shape[0], dtype=jnp.int32)
    pattern = (spin_index[None, :] == columns[:, None]).astype(jnp.float32)
    twist_real = (phases == 0).astype(jnp.float32) - (phases == 2).astype(jnp.float32)
    twist_imaginary = (phases == 1).astype(jnp.float32) - (phases == 3).astype(jnp.float32)
    return pattern * twist_real[:, None], pattern * twist_imaginary[:, None]


def sink_side(block_real, block_imaginary, element, gamma_real, gamma_imaginary):
    vectors = element.shape[0]
    full_width = block_real.shape[0]
    spin_count = full_width // vectors
    element_real = element[:, :vectors]
    element_imaginary = element[:, vectors:]
    rows_real = block_real.reshape(full_width * spin_count, vectors)
    rows_imaginary = block_imaginary.reshape(full_width * spin_count, vectors)
    inner_real = jnp.dot(rows_real, element_real.T, preferred_element_type=jnp.float32) - jnp.dot(rows_imaginary, element_imaginary.T, preferred_element_type=jnp.float32)
    inner_imaginary = jnp.dot(rows_real, element_imaginary.T, preferred_element_type=jnp.float32) + jnp.dot(rows_imaginary, element_real.T, preferred_element_type=jnp.float32)
    inner_real = inner_real.reshape(full_width, spin_count, vectors)
    inner_imaginary = inner_imaginary.reshape(full_width, spin_count, vectors)
    mixed_real = jnp.einsum("ab,cbe->cae", gamma_real, inner_real) - jnp.einsum("ab,cbe->cae", gamma_imaginary, inner_imaginary)
    mixed_imaginary = jnp.einsum("ab,cbe->cae", gamma_real, inner_imaginary) + jnp.einsum("ab,cbe->cae", gamma_imaginary, inner_real)
    return (mixed_real.reshape(full_width, full_width).astype(jnp.bfloat16),
            mixed_imaginary.reshape(full_width, full_width).astype(jnp.bfloat16))


def source_side(block_real, block_imaginary, element, gamma_real, gamma_imaginary):
    vectors = element.shape[0]
    full_width = block_real.shape[0]
    spin_count = full_width // vectors
    element_real = element[:, :vectors].astype(jnp.float32)
    element_imaginary = element[:, vectors:].astype(jnp.float32)
    stack_real = block_real.reshape(spin_count, vectors, full_width).astype(jnp.float32)
    stack_imaginary = block_imaginary.reshape(spin_count, vectors, full_width).astype(jnp.float32)
    mixed_real = jnp.einsum("xj,bjs->bxs", element_real, stack_real) + jnp.einsum("xj,bjs->bxs", element_imaginary, stack_imaginary)
    mixed_imaginary = jnp.einsum("xj,bjs->bxs", element_imaginary, stack_real) - jnp.einsum("xj,bjs->bxs", element_real, stack_imaginary)
    chirality = 1.0 - 2.0 * (jnp.arange(spin_count) >= spin_count // 2).astype(jnp.float32)
    column_signs = jnp.repeat(chirality, vectors)
    sign_table = chirality[:, None, None] * column_signs[None, None, :]
    mixed_real = mixed_real * sign_table
    mixed_imaginary = mixed_imaginary * sign_table
    final_real = jnp.einsum("ab,bxs->axs", gamma_real, mixed_real) - jnp.einsum("ab,bxs->axs", gamma_imaginary, mixed_imaginary)
    final_imaginary = jnp.einsum("ab,bxs->axs", gamma_real, mixed_imaginary) + jnp.einsum("ab,bxs->axs", gamma_imaginary, mixed_real)
    return (final_real.reshape(full_width, full_width).astype(jnp.bfloat16),
            final_imaginary.reshape(full_width, full_width).astype(jnp.bfloat16))


def pair_value(block, sink_elements, source_elements, gammas):
    full_width = block.shape[0]
    block_real = block[:, :full_width]
    block_imaginary = block[:, full_width:]
    values_real = []
    values_imaginary = []
    for family in range(sink_elements.shape[0]):
        meson_real = []
        meson_imaginary = []
        for member in range(2):
            sink_real, sink_imaginary = sink_side(block_real, block_imaginary, sink_elements[family, member], gammas[0], gammas[1])
            source_real, source_imaginary = source_side(block_real, block_imaginary, source_elements[family, 1 - member], gammas[2], gammas[3])
            meson_real.append(jnp.dot(sink_real.T, source_real, preferred_element_type=jnp.float32) - jnp.dot(sink_imaginary.T, source_imaginary, preferred_element_type=jnp.float32))
            meson_imaginary.append(jnp.dot(sink_real.T, source_imaginary, preferred_element_type=jnp.float32) + jnp.dot(sink_imaginary.T, source_real, preferred_element_type=jnp.float32))
        first_real = jnp.trace(meson_real[0])
        first_imaginary = jnp.trace(meson_imaginary[0])
        second_real = jnp.trace(meson_real[1])
        second_imaginary = jnp.trace(meson_imaginary[1])
        direct_real = first_real * second_real - first_imaginary * second_imaginary
        direct_imaginary = first_real * second_imaginary + first_imaginary * second_real
        box_real = jnp.sum(meson_real[0] * meson_real[1].T) - jnp.sum(meson_imaginary[0] * meson_imaginary[1].T)
        box_imaginary = jnp.sum(meson_real[0] * meson_imaginary[1].T) + jnp.sum(meson_imaginary[0] * meson_real[1].T)
        values_real.append((direct_real - box_real) * 0.0625)
        values_imaginary.append((direct_imaginary - box_imaginary) * 0.0625)
    return jnp.stack(values_real), jnp.stack(values_imaginary)


def reference(peramb, elementals, pair_times, pair_order, class_group, gamma_columns, gamma_phases):
    sink_gamma = gamma_matrix(gamma_columns[0], gamma_phases[0])
    source_gamma = gamma_matrix(gamma_columns[1], gamma_phases[1])
    gammas = (sink_gamma[0], sink_gamma[1], source_gamma[0], source_gamma[1])

    def one_slot(slot_index):
        chosen = pair_order[slot_index]
        block = lax.dynamic_index_in_dim(peramb, chosen, 0, keepdims=False)
        sink_time = pair_times[chosen, 0]
        source_time = pair_times[chosen, 1]
        sink_elements = lax.dynamic_index_in_dim(elementals, sink_time, 0, keepdims=False)
        source_elements = lax.dynamic_index_in_dim(elementals, source_time, 0, keepdims=False)
        value_real, value_imaginary = pair_value(block, sink_elements, source_elements, gammas)
        return jnp.stack([value_real, value_imaginary])

    values = lax.map(one_slot, jnp.arange(NPAIRS, dtype=jnp.int32))
    membership = (class_group[:, None] == jnp.arange(GROUPS, dtype=jnp.int32)[None, :]).astype(jnp.float32)
    summed = jnp.sum(values[:, :, :, None] * membership[None, None, :, :], axis=2)
    return jnp.transpose(summed, (1, 0, 2))
```

```python
import functools

import jax
import jax.numpy as jnp
from jax import lax
from jax.experimental import pallas as pl
from jax.experimental.pallas import tpu as pltpu
from jax.sharding import PartitionSpec as P

MESH = pl.DeviceIdType.MESH
F32 = jnp.float32
BF16 = jnp.bfloat16

NX, NZ, NY = 4, 8, 4
GROUPS = 8
SPINS = 4
VECTORS = 192
FULL = SPINS * VECTORS
ROWS = 24
PIECE = 384
PEERS = 16
STEPS = 4
EACH = PEERS // STEPS


def place():
    pair = lax.axis_index("pair")
    mom = lax.axis_index("mom")
    return pair // NZ, pair % NZ, mom // 2, mom % 2


def plane(pair):
    return {"pair": pair, "mom": lax.axis_index("mom")}


def column(y, core):
    return {"pair": lax.axis_index("pair"), "mom": y * 2 + core}


def copy_to(src, dst, send, recv, device):
    return pltpu.make_async_remote_copy(
        src_ref=src, dst_ref=dst, send_sem=send, recv_sem=recv, device_id=device, device_id_type=MESH
    )


def exchange_kernel(
    order, peramb, out, staged, picked, load_sem, self_sem, send_plane, send_ring, recv_plane,
    recv_up, recv_down, recv_far, send_core, recv_core,
):
    x, z, y, core = place()
    up, down = (y + 1) % NY, (y + NY - 1) % NY
    far = (y + 2) % NY
    other = 1 - core
    columns = pl.ds(pl.multiple_of(y * PIECE, 128), PIECE)
    load = pltpu.make_async_copy(peramb.at[:, :, columns], staged, load_sem)
    load.start()

    def target(j):
        dx, dz = j // 4, 2 * (j % 4) + core
        return ((x + dx) % NX) * NZ + (z + dz) % NZ

    def source(j):
        dx, dz = j // 4, 2 * (j % 4) + core
        return ((x + NX - dx) % NX) * NZ + (z + NZ - dz) % NZ

    barrier = pltpu.get_barrier_semaphore()
    for j in range(1, PEERS):
        pl.semaphore_signal(barrier, inc=1, device_id=plane(source(j)), device_id_type=MESH)
    @pl.when(core == 1)
    def _():
        pl.semaphore_signal(barrier, inc=1, device_id=plane(source(0)), device_id_type=MESH)
    for device in (column(up, core), column(down, core), column(y, other)):
        pl.semaphore_signal(barrier, inc=1, device_id=device, device_id_type=MESH)
    load.wait()
    pl.semaphore_wait(barrier, PEERS - 1 + 3 + core)

    for j in range(PEERS):
        picked[j] = staged[order[target(j)]]
        group = j // EACH
        if j == 0:
            @pl.when(core == 0)
            def _():
                pltpu.make_async_copy(picked.at[j], out.at[y, core, j], self_sem).start()
            @pl.when(core == 1)
            def _():
                copy_to(picked.at[j], out.at[y, core, j], self_sem, recv_plane.at[STEPS], plane(target(j))).start()
        else:
            copy_to(
                picked.at[j], out.at[y, core, j], send_plane.at[group], recv_plane.at[group], plane(target(j))
            ).start()

    def block(piece, side, g):
        return out.at[piece, side, pl.ds(g * EACH, EACH)]

    def to_other(piece, kind, g):
        copy_to(
            block(piece, core, g), block(piece, core, g), send_core.at[kind, g], recv_core.at[kind, g],
            column(y, other),
        ).start()

    def to_ring(piece, where, send, recv, g):
        copy_to(block(piece, core, g), block(piece, core, g), send, recv, column(where, core)).start()

    def arrived(piece, side, sem, g):
        pltpu.make_async_copy(block(piece, side, g), block(piece, side, g), sem).wait()

    def own(g):
        if g == 0:
            few = out.at[y, core, pl.ds(1, EACH - 1)]
            pltpu.make_async_copy(few, few, recv_plane.at[g]).wait()
            one = out.at[y, core, 0]
            @pl.when(core == 0)
            def _():
                pltpu.make_async_copy(one, one, self_sem).wait()
            @pl.when(core == 1)
            def _():
                pltpu.make_async_copy(one, one, recv_plane.at[STEPS]).wait()
        else:
            arrived(y, core, recv_plane.at[g], g)
        to_ring(y, up, send_ring.at[0, g], recv_up.at[g], g)
        to_ring(y, down, send_ring.at[1, g], recv_down.at[g], g)
        to_other(y, 0, g)

    def near(g):
        arrived(down, core, recv_up.at[g], g)
        if g % 2 == 0:
            to_ring(down, up, send_ring.at[2, g], recv_far.at[g], g)
        to_other(down, 1, g)
        arrived(up, core, recv_down.at[g], g)
        if g % 2 == 1:
            to_ring(up, down, send_ring.at[2, g], recv_far.at[g], g)
        to_other(up, 2, g)

    def last(g):
        arrived(far, core, recv_far.at[g], g)
        to_other(far, 3, g)

    for g in range(STEPS + 2):
        if g < STEPS:
            own(g)
        if 0 <= g - 1 < STEPS:
            near(g - 1)
        if 0 <= g - 2 < STEPS:
            last(g - 2)
    for g in range(STEPS):
        for kind, piece in enumerate((y, down, up, far)):
            arrived(piece, other, recv_core.at[kind, g], g)
            arrived(piece, core, send_core.at[kind, g], g)
        for kind in range(3):
            arrived(y, core, send_ring.at[kind, g], g)
        few = picked.at[pl.ds(1, EACH - 1)] if g == 0 else picked.at[pl.ds(g * EACH, EACH)]
        pltpu.make_async_copy(few, few, send_plane.at[g]).wait()
    @pl.when(core == 1)
    def _():
        pltpu.make_async_copy(picked.at[0], picked.at[0], self_sem).wait()


def exchange(order, peramb):
    return pl.pallas_call(
        exchange_kernel,
        out_shape=jax.ShapeDtypeStruct((NY, 2, PEERS, ROWS, PIECE), BF16),
        in_specs=[pl.BlockSpec(memory_space=pltpu.SMEM), pl.BlockSpec(memory_space=pl.ANY)],
        out_specs=pl.BlockSpec(memory_space=pltpu.VMEM),
        scratch_shapes=[
            pltpu.VMEM((NX * NZ, ROWS, PIECE), BF16),
            pltpu.VMEM((PEERS, ROWS, PIECE), BF16),
            pltpu.SemaphoreType.DMA,
            pltpu.SemaphoreType.DMA,
            pltpu.SemaphoreType.DMA((STEPS,)),
            pltpu.SemaphoreType.DMA((3, STEPS)),
            pltpu.SemaphoreType.DMA((STEPS + 1,)),
            pltpu.SemaphoreType.DMA((STEPS,)),
            pltpu.SemaphoreType.DMA((STEPS,)),
            pltpu.SemaphoreType.DMA((STEPS,)),
            pltpu.SemaphoreType.DMA((4, STEPS)),
            pltpu.SemaphoreType.DMA((4, STEPS)),
        ],
        compiler_params=pltpu.CompilerParams(
            collective_id=0, has_side_effects=True, vmem_limit_bytes=32 * 1024 * 1024
        ),
        name="exchange",
    )(order, peramb)


def phase_parts(phase):
    real = jnp.where(phase == 0, 1.0, jnp.where(phase == 2, -1.0, 0.0)).astype(F32)
    imaginary = jnp.where(phase == 1, 1.0, jnp.where(phase == 3, -1.0, 0.0)).astype(F32)
    return real, imaginary


def spin_phases(columns, phases, side):
    found = []
    for spin in range(SPINS):
        real = jnp.float32(0.0)
        imaginary = jnp.float32(0.0)
        for row in range(SPINS):
            one, two = phase_parts(phases[side, row])
            chirality = 1.0 if (row if side == 0 else spin) < SPINS // 2 else -1.0
            here = jnp.where(columns[side, row] == spin, chirality, 0.0).astype(F32)
            real += here * one
            imaginary += here * two
        found.append((real, imaginary))
    return found


def padded_elements(tile):
    first = tile[:, :256].astype(F32)
    second = tile[:, 128:].astype(F32)
    lane = lax.broadcasted_iota(jnp.int32, first.shape, 1)
    real_low = jnp.where(lane < VECTORS, first, 0.0)
    imaginary_high = jnp.where(lane >= 64, second, 0.0)
    real_high = pltpu.roll(real_low, 64, 1)
    imaginary_low = pltpu.roll(imaginary_high, VECTORS, 1)
    return (real_low, imaginary_low), (real_high, imaginary_high)


def prepare_left(elements, columns, phases, side, left):
    turns = spin_phases(columns, phases, side)
    for member in range(2):
        padded = padded_elements(elements(member if side == 0 else 1 - member))
        for spin in range(SPINS):
            real, imaginary = padded[spin % 2]
            one, two = turns[spin]
            turned_real = one * real - two * imaginary
            turned_imaginary = one * imaginary + two * real
            base = member * 2 * VECTORS
            upper, lower = pl.ds(base, VECTORS), pl.ds(base + VECTORS, VECTORS)
            left[spin, 0, upper, :] = turned_real.astype(BF16)
            left[spin, 0, lower, :] = turned_imaginary.astype(BF16)
            if side == 0:
                left[spin, 1, upper, :] = (-turned_imaginary).astype(BF16)
                left[spin, 1, lower, :] = turned_real.astype(BF16)
            else:
                left[spin, 1, upper, :] = turned_imaginary.astype(BF16)
                left[spin, 1, lower, :] = (-turned_real).astype(BF16)


def gather_rows(pieces, block, x, z):
    def position(s):
        dx, dz = (x + NX - s // NZ) % NX, (z + NZ - s % NZ) % NZ
        return dz % 2, dx * 4 + dz // 2

    def step(i, carry):
        one, two = position(2 * i), position(2 * i + 1)
        for piece in range(NY):
            a = pieces[piece, one[0], one[1]].astype(F32)
            b = pieces[piece, two[0], two[1]].astype(F32)
            rows = pl.ds(pl.multiple_of(i * 2 * ROWS, 16), 2 * ROWS)
            block[rows, piece * PIECE:(piece + 1) * PIECE] = jnp.concatenate([a, b], axis=0).astype(BF16)
        return carry

    lax.fori_loop(0, NX * NZ // 2, step, 0)


def product(left, right, dims):
    return lax.dot_general(left, right, (dims, ((), ())), preferred_element_type=F32)


def sides(block, sink_left, source_left, sink, source):
    for spin in range(SPINS):
        start = (spin // 2) * PIECE + (spin % 2) * 128
        turned = product(sink_left[spin, 0], block[:, start:start + 256], ((1,), (1,)))
        turned += product(sink_left[spin, 1], block[:, FULL + start:FULL + start + 256], ((1,), (1,)))
        turned = turned.astype(BF16)
        for member in range(2):
            base = member * 2 * VECTORS
            sink[member, spin, :, :FULL] = turned[base:base + VECTORS]
            sink[member, spin, :, FULL:] = turned[base + VECTORS:base + 2 * VECTORS]
    for spin in range(SPINS):
        start = (spin // 2) * PIECE + (spin % 2) * 128
        turned = product(source_left[spin, 0], block[start:start + 256, :FULL], ((1,), (0,)))
        turned += product(source_left[spin, 1], block[start:start + 256, FULL:], ((1,), (0,)))
        for member in range(2):
            base = member * 2 * VECTORS
            real = turned[base:base + VECTORS]
            imaginary = turned[base + VECTORS:base + 2 * VECTORS]
            source[member, 0, spin, :, :FULL] = real.astype(BF16)
            source[member, 0, spin, :, FULL:] = imaginary.astype(BF16)
            source[member, 1, spin, :, :FULL] = (-imaginary).astype(BF16)
            source[member, 1, spin, :, FULL:] = real.astype(BF16)


def mesons(columns, sink, source, meson):
    width = 256
    for member in range(2):
        left = jnp.concatenate([sink[member, columns[0, spin]] for spin in range(SPINS)], axis=0)

        def step(n, carry):
            at = pl.ds(pl.multiple_of(n * width, 128), width)
            right = jnp.concatenate(
                [source[member, part, columns[1, spin], :, at] for part in range(2) for spin in range(SPINS)], axis=0
            )
            meson[member, :, at] = product(left, right, ((1,), (0,)))
            return carry

        lax.fori_loop(0, 2 * FULL // width, step, 0)


def slot_value(meson):
    tile = 128
    count = FULL // tile
    eye = (
        lax.broadcasted_iota(jnp.int32, (tile, tile), 0) == lax.broadcasted_iota(jnp.int32, (tile, tile), 1)
    ).astype(F32)
    traces = []
    for member in range(2):
        for part in range(2):
            total = jnp.zeros((tile, tile), F32)
            for i in range(count):
                total += eye * meson[member, i * tile:(i + 1) * tile, part * FULL + i * tile:part * FULL + (i + 1) * tile]
            traces.append(jnp.sum(total))

    def step(i, carry):
        box_real, box_imaginary = carry
        rows = pl.ds(pl.multiple_of(i * tile, tile), tile)
        for j in range(count):
            here = slice(j * tile, (j + 1) * tile)
            first_real = meson[0, rows, here]
            first_imaginary = meson[0, rows, FULL + j * tile:FULL + (j + 1) * tile]
            second_real = meson[1, here, rows].T
            second_imaginary = meson[1, here, pl.ds(pl.multiple_of(FULL + i * tile, tile), tile)].T
            box_real += first_real * second_real - first_imaginary * second_imaginary
            box_imaginary += first_real * second_imaginary + first_imaginary * second_real
        return box_real, box_imaginary

    zero = jnp.zeros((tile, tile), F32)
    box_real, box_imaginary = lax.fori_loop(0, count, step, (zero, zero))
    one_real, one_imaginary, two_real, two_imaginary = traces
    direct_real = one_real * two_real - one_imaginary * two_imaginary
    direct_imaginary = one_real * two_imaginary + one_imaginary * two_real
    return (direct_real - jnp.sum(box_real)) * 0.0625, (direct_imaginary - jnp.sum(box_imaginary)) * 0.0625


def contract_kernel(
    order, times, columns, phases, position, pieces, elements, value, block, sink_left, source_left, sink, source,
    meson, held, sems,
):
    x, z = position[0], position[1]
    chosen = order[position[0] * NZ + position[1]]
    loads = [pltpu.make_async_copy(elements.at[times[chosen, side], 0], held.at[side], sems.at[side]) for side in range(2)]
    for load in loads:
        load.start()
    gather_rows(pieces, block, x, z)
    for load in loads:
        load.wait()
    prepare_left(lambda member: held[0, member], columns, phases, 0, sink_left)
    prepare_left(lambda member: held[1, member], columns, phases, 1, source_left)
    sides(block, sink_left, source_left, sink, source)
    mesons(columns, sink, source, meson)
    real, imaginary = slot_value(meson)
    row = lax.broadcasted_iota(jnp.int32, (8, 128), 0)
    value[...] = jnp.where(row == 0, real, jnp.where(row == 1, imaginary, 0.0))


def contract(order, times, columns, phases, position, pieces, elements):
    smem = pl.BlockSpec(memory_space=pltpu.SMEM)
    return pl.pallas_call(
        contract_kernel,
        out_shape=jax.ShapeDtypeStruct((8, 128), F32),
        in_specs=[smem] * 5 + [pl.BlockSpec(memory_space=pltpu.VMEM), pl.BlockSpec(memory_space=pl.ANY)],
        out_specs=pl.BlockSpec(memory_space=pltpu.VMEM),
        scratch_shapes=[
            pltpu.VMEM((FULL, 2 * FULL), BF16),
            pltpu.VMEM((SPINS, 2, FULL, 256), BF16),
            pltpu.VMEM((SPINS, 2, FULL, 256), BF16),
            pltpu.VMEM((2, SPINS, VECTORS, 2 * FULL), BF16),
            pltpu.VMEM((2, 2, SPINS, VECTORS, 2 * FULL), BF16),
            pltpu.VMEM((2, FULL, 2 * FULL), F32),
            pltpu.VMEM((2, 2, VECTORS, 2 * VECTORS), BF16),
            pltpu.SemaphoreType.DMA((2,)),
        ],
        compiler_params=pltpu.CompilerParams(vmem_limit_bytes=56 * 1024 * 1024),
        name="contract",
    )(order, times, columns, phases, position, pieces, elements)


def per_device(peramb, elementals, pair_times, pair_order, class_group, gamma_columns, gamma_phases):
    pieces = exchange(pair_order, peramb)
    pair = lax.axis_index("pair")
    position = jnp.stack([pair // NZ, pair % NZ]).astype(jnp.int32)
    value = contract(pair_order, pair_times, gamma_columns, gamma_phases, position, pieces, elementals)
    membership = (class_group[0] == jnp.arange(GROUPS, dtype=jnp.int32)).astype(F32)
    partial = value[:2, :1, None].reshape(2, 1, 1) * membership[None, None, :]
    return lax.psum(partial, "mom")


def solution(mesh):
    placed = (P(None, "pair", None), P(None, "mom", None, None, None), P(), P(), P("mom"), P(), P())
    return jax.shard_map(
        per_device, mesh=mesh, in_specs=placed, out_specs=P(None, "pair", None), check_vma=False
    )
```

```python
import jax
import jax.numpy as jnp
from jax import lax
from jax.experimental import pallas as pl
from jax.experimental.pallas import tpu as pltpu
from jax.sharding import PartitionSpec as P

MESH = pl.DeviceIdType.MESH
F32 = jnp.float32
BF16 = jnp.bfloat16

NX, NZ, NY = 4, 8, 4
GROUPS = 8
SPINS = 4
VECTORS = 192
FULL = SPINS * VECTORS
ROWS = 24
PIECE = 384
PEERS = 16


def place():
    pair = lax.axis_index("pair")
    mom = lax.axis_index("mom")
    return pair // NZ, pair % NZ, mom // 2, mom % 2


def plane(pair):
    return {"pair": pair, "mom": lax.axis_index("mom")}


def column(y, core):
    return {"pair": lax.axis_index("pair"), "mom": y * 2 + core}


def copy_to(src, dst, send, recv, device):
    return pltpu.make_async_remote_copy(
        src_ref=src, dst_ref=dst, send_sem=send, recv_sem=recv, device_id=device, device_id_type=MESH
    )


def phase_parts(phase):
    real = jnp.where(phase == 0, 1.0, jnp.where(phase == 2, -1.0, 0.0)).astype(F32)
    imaginary = jnp.where(phase == 1, 1.0, jnp.where(phase == 3, -1.0, 0.0)).astype(F32)
    return real, imaginary


def spin_phases(columns, phases, side):
    found = []
    for spin in range(SPINS):
        real = jnp.float32(0.0)
        imaginary = jnp.float32(0.0)
        for row in range(SPINS):
            one, two = phase_parts(phases[side, row])
            chirality = 1.0 if (row if side == 0 else spin) < SPINS // 2 else -1.0
            here = jnp.where(columns[side, row] == spin, chirality, 0.0).astype(F32)
            real += here * one
            imaginary += here * two
        found.append((real, imaginary))
    return found


def padded_elements(tile):
    first = tile[:, :256].astype(F32)
    second = tile[:, 128:].astype(F32)
    lane = lax.broadcasted_iota(jnp.int32, first.shape, 1)
    real_low = jnp.where(lane < VECTORS, first, 0.0)
    imaginary_high = jnp.where(lane >= 64, second, 0.0)
    real_high = pltpu.roll(real_low, 64, 1)
    imaginary_low = pltpu.roll(imaginary_high, VECTORS, 1)
    return (real_low, imaginary_low), (real_high, imaginary_high)


def prepare_left(elements, columns, phases, side, left):
    turns = spin_phases(columns, phases, side)
    for member in range(2):
        padded = padded_elements(elements(member if side == 0 else 1 - member))
        for spin in range(SPINS):
            real, imaginary = padded[spin % 2]
            one, two = turns[spin]
            turned_real = one * real - two * imaginary
            turned_imaginary = one * imaginary + two * real
            base = member * 2 * VECTORS
            upper, lower = pl.ds(base, VECTORS), pl.ds(base + VECTORS, VECTORS)
            left[spin, 0, upper, :] = turned_real.astype(BF16)
            left[spin, 0, lower, :] = turned_imaginary.astype(BF16)
            if side == 0:
                left[spin, 1, upper, :] = (-turned_imaginary).astype(BF16)
                left[spin, 1, lower, :] = turned_real.astype(BF16)
            else:
                left[spin, 1, upper, :] = turned_imaginary.astype(BF16)
                left[spin, 1, lower, :] = (-turned_real).astype(BF16)


def gather_rows(pieces, block, x, z):
    def position(s):
        dx, dz = (x + NX - s // NZ) % NX, (z + NZ - s % NZ) % NZ
        return dz % 2, dx * 4 + dz // 2

    def step(i, carry):
        one, two = position(2 * i), position(2 * i + 1)
        for piece in range(NY):
            a = pieces[piece, one[0], one[1]].astype(F32)
            b = pieces[piece, two[0], two[1]].astype(F32)
            rows = pl.ds(pl.multiple_of(i * 2 * ROWS, 16), 2 * ROWS)
            block[rows, piece * PIECE:(piece + 1) * PIECE] = jnp.concatenate([a, b], axis=0).astype(BF16)
        return carry

    lax.fori_loop(0, NX * NZ // 2, step, 0)


def product(left, right, dims):
    return lax.dot_general(left, right, (dims, ((), ())), preferred_element_type=F32)


def sides(block, sink_left, source_left, sink, source):
    for spin in range(SPINS):
        start = (spin // 2) * PIECE + (spin % 2) * 128
        turned = product(sink_left[spin, 0], block[:, start:start + 256], ((1,), (1,)))
        turned += product(sink_left[spin, 1], block[:, FULL + start:FULL + start + 256], ((1,), (1,)))
        turned = turned.astype(BF16)
        for member in range(2):
            base = member * 2 * VECTORS
            sink[member, spin, :, :FULL] = turned[base:base + VECTORS]
            sink[member, spin, :, FULL:] = turned[base + VECTORS:base + 2 * VECTORS]
    for spin in range(SPINS):
        start = (spin // 2) * PIECE + (spin % 2) * 128
        turned = product(source_left[spin, 0], block[start:start + 256, :FULL], ((1,), (0,)))
        turned += product(source_left[spin, 1], block[start:start + 256, FULL:], ((1,), (0,)))
        for member in range(2):
            base = member * 2 * VECTORS
            real = turned[base:base + VECTORS]
            imaginary = turned[base + VECTORS:base + 2 * VECTORS]
            source[member, 0, spin, :, :FULL] = real.astype(BF16)
            source[member, 0, spin, :, FULL:] = imaginary.astype(BF16)
            source[member, 1, spin, :, :FULL] = (-imaginary).astype(BF16)
            source[member, 1, spin, :, FULL:] = real.astype(BF16)


def mesons(columns, sink, source, meson):
    width = 256
    for member in range(2):
        left = jnp.concatenate([sink[member, columns[0, spin]] for spin in range(SPINS)], axis=0)

        def step(n, carry):
            at = pl.ds(pl.multiple_of(n * width, 128), width)
            right = jnp.concatenate(
                [source[member, part, columns[1, spin], :, at] for part in range(2) for spin in range(SPINS)], axis=0
            )
            meson[member, :, at] = product(left, right, ((1,), (0,)))
            return carry

        lax.fori_loop(0, 2 * FULL // width, step, 0)


def slot_value(meson):
    tile = 128
    count = FULL // tile
    eye = (
        lax.broadcasted_iota(jnp.int32, (tile, tile), 0) == lax.broadcasted_iota(jnp.int32, (tile, tile), 1)
    ).astype(F32)
    traces = []
    for member in range(2):
        for part in range(2):
            total = jnp.zeros((tile, tile), F32)
            for i in range(count):
                total += eye * meson[member, i * tile:(i + 1) * tile, part * FULL + i * tile:part * FULL + (i + 1) * tile]
            traces.append(jnp.sum(total))

    def step(i, carry):
        box_real, box_imaginary = carry
        rows = pl.ds(pl.multiple_of(i * tile, tile), tile)
        for j in range(count):
            here = slice(j * tile, (j + 1) * tile)
            first_real = meson[0, rows, here]
            first_imaginary = meson[0, rows, FULL + j * tile:FULL + (j + 1) * tile]
            second_real = meson[1, here, rows].T
            second_imaginary = meson[1, here, pl.ds(pl.multiple_of(FULL + i * tile, tile), tile)].T
            box_real += first_real * second_real - first_imaginary * second_imaginary
            box_imaginary += first_real * second_imaginary + first_imaginary * second_real
        return box_real, box_imaginary

    zero = jnp.zeros((tile, tile), F32)
    box_real, box_imaginary = lax.fori_loop(0, count, step, (zero, zero))
    one_real, one_imaginary, two_real, two_imaginary = traces
    direct_real = one_real * two_real - one_imaginary * two_imaginary
    direct_imaginary = one_real * two_imaginary + one_imaginary * two_real
    return (direct_real - jnp.sum(box_real)) * 0.0625, (direct_imaginary - jnp.sum(box_imaginary)) * 0.0625


def correlator_kernel(
    order, times, columns, phases, group, peramb, elementals, out, staged_own, staged_far, picked, pieces, held, block,
    sink_left, source_left, sink, source, meson, votes, load_sem, self_sem, send_plane, recv_plane, send_ring,
    recv_ring, send_core, recv_core, send_vote, recv_vote,
):
    x, z, y, core = place()
    mom = lax.axis_index("mom")
    up, down, far = (y + 1) % NY, (y + NY - 1) % NY, (y + 2) % NY
    other = 1 - core

    def target(j):
        dx, dz = j // 4, 2 * (j % 4) + core
        return ((x + dx) % NX) * NZ + (z + dz) % NZ

    def source_of(j):
        dx, dz = j // 4, 2 * (j % 4) + core
        return ((x + NX - dx) % NX) * NZ + (z + NZ - dz) % NZ

    def peer(step):
        return {"pair": lax.axis_index("pair"), "mom": (mom + step) % (2 * NY)}

    staged = (staged_own, staged_far)
    loads = []
    for phase, piece in enumerate((y, far)):
        at = pl.ds(pl.multiple_of(piece * PIECE, 128), PIECE)
        loads.append(pltpu.make_async_copy(peramb.at[:, :, at], staged[phase], load_sem.at[phase]))
    loads.append(pltpu.make_async_copy(elementals, held, load_sem.at[2]))
    for load in loads:
        load.start()

    barrier = pltpu.get_barrier_semaphore()
    for j in range(1, PEERS):
        pl.semaphore_signal(barrier, inc=1, device_id=plane(source_of(j)), device_id_type=MESH)
    @pl.when(core == 1)
    def _():
        pl.semaphore_signal(barrier, inc=1, device_id=plane(source_of(0)), device_id_type=MESH)
    for step in range(1, 2 * NY):
        pl.semaphore_signal(barrier, inc=1, device_id=peer(step), device_id_type=MESH)
    loads[0].wait()
    pl.semaphore_wait(barrier, PEERS - 1 + 2 * NY - 1 + core)

    def pick(phase):
        for j in range(PEERS):
            picked[phase, j] = staged[phase][order[target(j)]]

    def send_in_plane(phase, piece):
        for j in range(PEERS):
            src, dst = picked.at[phase, j], pieces.at[piece, core, j]
            if j == 0:
                @pl.when(core == 0)
                def _():
                    pltpu.make_async_copy(src, dst, recv_plane.at[phase]).start()
                @pl.when(core == 1)
                def _():
                    copy_to(src, dst, self_sem.at[phase], recv_plane.at[phase], plane(target(j))).start()
            else:
                copy_to(src, dst, send_plane.at[phase], recv_plane.at[phase], plane(target(j))).start()

    def sent_in_plane(phase):
        most = picked.at[phase, pl.ds(1, PEERS - 1)]
        pltpu.make_async_copy(most, most, send_plane.at[phase]).wait()
        @pl.when(core == 1)
        def _():
            one = picked.at[phase, 0]
            pltpu.make_async_copy(one, one, self_sem.at[phase]).wait()

    def finish(piece, side, sem):
        part = pieces.at[piece, side]
        pltpu.make_async_copy(part, part, sem).wait()

    def to_ring(way, where):
        part = pieces.at[y, core]
        copy_to(part, part, send_ring.at[way], recv_ring.at[way], column(where, core)).start()

    def to_other(kind, piece):
        part = pieces.at[piece, core]
        copy_to(part, part, send_core.at[kind], recv_core.at[kind], column(y, other)).start()

    pick(0)
    send_in_plane(0, y)
    loads[1].wait()
    pick(1)
    loads[2].wait()
    chosen = order[lax.axis_index("pair")]
    prepare_left(lambda member: held[times[0, chosen], 0, member], columns, phases, 0, sink_left)
    prepare_left(lambda member: held[times[1, chosen], 0, member], columns, phases, 1, source_left)

    finish(y, core, recv_plane.at[0])
    to_ring(0, up)
    to_ring(1, down)
    send_in_plane(1, far)
    to_other(0, y)
    finish(y, other, recv_core.at[0])
    finish(down, core, recv_ring.at[0])
    to_other(1, down)
    finish(up, core, recv_ring.at[1])
    to_other(2, up)
    finish(far, core, recv_plane.at[1])
    to_other(3, far)
    finish(down, other, recv_core.at[1])
    finish(up, other, recv_core.at[2])
    finish(far, other, recv_core.at[3])

    gather_rows(pieces, block, x, z)
    sides(block, sink_left, source_left, sink, source)
    mesons(columns, sink, source, meson)
    real, imaginary = slot_value(meson)

    row = lax.broadcasted_iota(jnp.int32, (8, 128), 0)
    lane = lax.broadcasted_iota(jnp.int32, (8, 128), 1)
    both = jnp.where(row == 0, real, jnp.where(row == 1, imaginary, 0.0))
    votes[mom] = jnp.where(lane == group[0], both, 0.0)
    for step in range(1, 2 * NY):
        copy_to(votes.at[mom], votes.at[mom], send_vote.at[step], recv_vote.at[step], peer(step)).start()

    sent_in_plane(0)
    sent_in_plane(1)
    for way in range(2):
        finish(y, core, send_ring.at[way])
    for kind, piece in enumerate((y, down, up, far)):
        finish(piece, core, send_core.at[kind])
    for step in range(1, 2 * NY):
        sender = (mom + 2 * NY - step) % (2 * NY)
        pltpu.make_async_copy(votes.at[sender], votes.at[sender], recv_vote.at[step]).wait()
    total = votes[0]
    for each in range(1, 2 * NY):
        total = total + votes[each]
    out[0] = total[0:1, :GROUPS]
    out[1] = total[1:2, :GROUPS]
    for step in range(1, 2 * NY):
        pltpu.make_async_copy(votes.at[mom], votes.at[mom], send_vote.at[step]).wait()


def per_device(peramb, elementals, pair_times, pair_order, class_group, gamma_columns, gamma_phases):
    smem = pl.BlockSpec(memory_space=pltpu.SMEM)
    anywhere = pl.BlockSpec(memory_space=pl.ANY)
    dma = pltpu.SemaphoreType.DMA
    return pl.pallas_call(
        correlator_kernel,
        out_shape=jax.ShapeDtypeStruct((2, 1, GROUPS), F32),
        in_specs=[smem] * 5 + [anywhere] * 2,
        out_specs=pl.BlockSpec(memory_space=pltpu.VMEM),
        scratch_shapes=[
            pltpu.VMEM((NX * NZ, ROWS, PIECE), BF16),
            pltpu.VMEM((NX * NZ, ROWS, PIECE), BF16),
            pltpu.VMEM((2, PEERS, ROWS, PIECE), BF16),
            pltpu.VMEM((NY, 2, PEERS, ROWS, PIECE), BF16),
            pltpu.VMEM(elementals.shape, BF16),
            pltpu.VMEM((FULL, 2 * FULL), BF16),
            pltpu.VMEM((SPINS, 2, FULL, 256), BF16),
            pltpu.VMEM((SPINS, 2, FULL, 256), BF16),
            pltpu.VMEM((2, SPINS, VECTORS, 2 * FULL), BF16),
            pltpu.VMEM((2, 2, SPINS, VECTORS, 2 * FULL), BF16),
            pltpu.VMEM((2, FULL, 2 * FULL), F32),
            pltpu.VMEM((2 * NY, 8, 128), F32),
            dma((3,)),
            dma((2,)),
            dma((2,)),
            dma((2,)),
            dma((2,)),
            dma((2,)),
            dma((4,)),
            dma((4,)),
            dma((2 * NY,)),
            dma((2 * NY,)),
        ],
        compiler_params=pltpu.CompilerParams(
            collective_id=0, has_side_effects=True, vmem_limit_bytes=60 * 1024 * 1024
        ),
        cost_estimate=pl.CostEstimate(flops=11_000_000_000, bytes_accessed=8_000_000, transcendentals=0),
        name="correlator",
    )(pair_order, pair_times.T, gamma_columns, gamma_phases, class_group, peramb, elementals)


def solution(mesh):
    placed = (P(None, "pair", None), P(None, "mom", None, None, None), P(), P(), P("mom"), P(), P())
    return jax.shard_map(
        per_device, mesh=mesh, in_specs=placed, out_specs=P(None, "pair", None), check_vma=False
    )
```

```python
import jax
import jax.numpy as jnp
from jax import lax
from jax.experimental import pallas as pl
from jax.experimental.pallas import tpu as pltpu
from jax.sharding import PartitionSpec as P

MESH = pl.DeviceIdType.MESH
F32 = jnp.float32
BF16 = jnp.bfloat16

NX, NZ, NY = 4, 8, 4
GROUPS = 8
SPINS = 4
VECTORS = 192
FULL = SPINS * VECTORS
ROWS = 24
PIECE = 384
PEERS = 16


def place():
    pair = lax.axis_index("pair")
    mom = lax.axis_index("mom")
    return pair // NZ, pair % NZ, mom // 2, mom % 2


def plane(pair):
    return {"pair": pair, "mom": lax.axis_index("mom")}


def column(y, core):
    return {"pair": lax.axis_index("pair"), "mom": y * 2 + core}


def copy_to(src, dst, send, recv, device):
    return pltpu.make_async_remote_copy(
        src_ref=src, dst_ref=dst, send_sem=send, recv_sem=recv, device_id=device, device_id_type=MESH
    )


def phase_parts(phase):
    real = jnp.where(phase == 0, 1.0, jnp.where(phase == 2, -1.0, 0.0)).astype(F32)
    imaginary = jnp.where(phase == 1, 1.0, jnp.where(phase == 3, -1.0, 0.0)).astype(F32)
    return real, imaginary


def spin_phases(columns, phases, side):
    found = []
    for spin in range(SPINS):
        real = jnp.float32(0.0)
        imaginary = jnp.float32(0.0)
        for row in range(SPINS):
            one, two = phase_parts(phases[side, row])
            chirality = 1.0 if (row if side == 0 else spin) < SPINS // 2 else -1.0
            here = jnp.where(columns[side, row] == spin, chirality, 0.0).astype(F32)
            real += here * one
            imaginary += here * two
        found.append((real, imaginary))
    return found


def padded_elements(tile):
    first = tile[:, :256].astype(F32)
    second = tile[:, 128:].astype(F32)
    lane = lax.broadcasted_iota(jnp.int32, first.shape, 1)
    real_low = jnp.where(lane < VECTORS, first, 0.0)
    imaginary_high = jnp.where(lane >= 64, second, 0.0)
    real_high = pltpu.roll(real_low, 64, 1)
    imaginary_low = pltpu.roll(imaginary_high, VECTORS, 1)
    return (real_low, imaginary_low), (real_high, imaginary_high)


def prepare_left(elements, columns, phases, side, left):
    turns = spin_phases(columns, phases, side)
    for member in range(2):
        padded = padded_elements(elements(member if side == 0 else 1 - member))
        for spin in range(SPINS):
            real, imaginary = padded[spin % 2]
            one, two = turns[spin]
            turned_real = one * real - two * imaginary
            turned_imaginary = one * imaginary + two * real
            base = member * 2 * VECTORS
            upper, lower = pl.ds(base, VECTORS), pl.ds(base + VECTORS, VECTORS)
            left[spin, 0, upper, :] = turned_real.astype(BF16)
            left[spin, 0, lower, :] = turned_imaginary.astype(BF16)
            if side == 0:
                left[spin, 1, upper, :] = (-turned_imaginary).astype(BF16)
                left[spin, 1, lower, :] = turned_real.astype(BF16)
            else:
                left[spin, 1, upper, :] = turned_imaginary.astype(BF16)
                left[spin, 1, lower, :] = (-turned_real).astype(BF16)


def gather_rows(pieces, block, x, z):
    def position(s):
        dx, dz = (x + NX - s // NZ) % NX, (z + NZ - s % NZ) % NZ
        return dz % 2, dx * 4 + dz // 2

    def step(i, carry):
        one, two = position(2 * i), position(2 * i + 1)
        for piece in range(NY):
            a = pieces[piece, one[0], one[1]].astype(F32)
            b = pieces[piece, two[0], two[1]].astype(F32)
            rows = pl.ds(pl.multiple_of(i * 2 * ROWS, 16), 2 * ROWS)
            block[rows, piece * PIECE:(piece + 1) * PIECE] = jnp.concatenate([a, b], axis=0).astype(BF16)
        return carry

    lax.fori_loop(0, NX * NZ // 2, step, 0)


def product(left, right, dims):
    return lax.dot_general(left, right, (dims, ((), ())), preferred_element_type=F32)


def triple(real, imaginary, sign):
    real, imaginary = real.astype(BF16), imaginary.astype(BF16)
    one, two = real.astype(F32), imaginary.astype(F32)
    return real, imaginary, (one + two).astype(BF16), None if sign == 0 else (two - one).astype(BF16)


def sides(block, sink_left, source_left, sink, source):
    for spin in range(SPINS):
        start = (spin // 2) * PIECE + (spin % 2) * 128
        turned = product(sink_left[spin, 0], block[:, start:start + 256], ((1,), (1,)))
        turned += product(sink_left[spin, 1], block[:, FULL + start:FULL + start + 256], ((1,), (1,)))
        for member in range(2):
            base = member * 2 * VECTORS
            real, imaginary, both, _ = triple(turned[base:base + VECTORS], turned[base + VECTORS:base + 2 * VECTORS], 0)
            sink[member, spin, :, :FULL] = both
            sink[member, spin, :, FULL:2 * FULL] = real
            sink[member, spin, :, 2 * FULL:] = imaginary
    for spin in range(SPINS):
        start = (spin // 2) * PIECE + (spin % 2) * 128
        turned = product(source_left[spin, 0], block[start:start + 256, :FULL], ((1,), (0,)))
        turned += product(source_left[spin, 1], block[start:start + 256, FULL:], ((1,), (0,)))
        for member in range(2):
            base = member * 2 * VECTORS
            real, _, both, less = triple(turned[base:base + VECTORS], turned[base + VECTORS:base + 2 * VECTORS], 1)
            source[member, spin, :, :FULL] = real
            source[member, spin, :, FULL:2 * FULL] = less
            source[member, spin, :, 2 * FULL:] = both


WIDTH = 256


def meson_columns(columns, sink, source, member, n):
    found = []
    for part in range(3):
        left = jnp.concatenate(
            [sink[member, columns[0, spin], :, part * FULL:(part + 1) * FULL] for spin in range(SPINS)], axis=0
        )
        start = part * FULL + n * WIDTH
        right = jnp.concatenate(
            [source[member, columns[1, spin], :, start:start + WIDTH] for spin in range(SPINS)], axis=0
        )
        found.append(product(left, right, ((1,), (0,))))
    return found[0] - found[2], found[0] + found[1]


def folded(tile):
    return jnp.sum(tile.reshape(-1, 8, tile.shape[1]), axis=0)


def slot_value(columns, sink, source, flipped):
    eye = (
        lax.broadcasted_iota(jnp.int32, (WIDTH, WIDTH), 0) == lax.broadcasted_iota(jnp.int32, (WIDTH, WIDTH), 1)
    )
    zero = jnp.zeros((8, WIDTH), F32)
    traces = [[zero, zero], [zero, zero]]
    box_real = box_imaginary = zero
    for member in (1, 0):
        for n in range(FULL // WIDTH):
            at = slice(n * WIDTH, (n + 1) * WIDTH)
            parts = meson_columns(columns, sink, source, member, n)
            for part in range(2):
                traces[member][part] += folded(jnp.where(eye, parts[part][at], 0.0))
            if member == 1:
                for part in range(2):
                    flipped[part, at, :] = parts[part].T
            else:
                real, imaginary = parts
                box_real += folded(real * flipped[0, :, at] - imaginary * flipped[1, :, at])
                box_imaginary += folded(real * flipped[1, :, at] + imaginary * flipped[0, :, at])
    one_real, one_imaginary = (jnp.sum(part) for part in traces[0])
    two_real, two_imaginary = (jnp.sum(part) for part in traces[1])
    direct_real = one_real * two_real - one_imaginary * two_imaginary
    direct_imaginary = one_real * two_imaginary + one_imaginary * two_real
    return (direct_real - jnp.sum(box_real)) * 0.0625, (direct_imaginary - jnp.sum(box_imaginary)) * 0.0625


def correlator_kernel(
    order, times, columns, phases, group, peramb, elementals, out, staged_own, staged_far, picked, pieces, held, block,
    sink_left, source_left, sink, source, flipped, votes, load_sem, self_sem, send_plane, recv_plane, send_ring,
    recv_ring, send_core, recv_core, send_vote, recv_vote,
):
    x, z, y, core = place()
    mom = lax.axis_index("mom")
    up, down, far = (y + 1) % NY, (y + NY - 1) % NY, (y + 2) % NY
    other = 1 - core

    def target(j):
        dx, dz = j // 4, 2 * (j % 4) + core
        return ((x + dx) % NX) * NZ + (z + dz) % NZ

    def source_of(j):
        dx, dz = j // 4, 2 * (j % 4) + core
        return ((x + NX - dx) % NX) * NZ + (z + NZ - dz) % NZ

    def peer(step):
        return {"pair": lax.axis_index("pair"), "mom": (mom + step) % (2 * NY)}

    staged = (staged_own, staged_far)
    loads = []
    for phase, piece in enumerate((y, far)):
        at = pl.ds(pl.multiple_of(piece * PIECE, 128), PIECE)
        loads.append(pltpu.make_async_copy(peramb.at[:, :, at], staged[phase], load_sem.at[phase]))
    loads.append(pltpu.make_async_copy(elementals, held, load_sem.at[2]))
    for load in loads:
        load.start()

    barrier = pltpu.get_barrier_semaphore()
    for j in range(1, PEERS):
        pl.semaphore_signal(barrier, inc=1, device_id=plane(source_of(j)), device_id_type=MESH)
    @pl.when(core == 1)
    def _():
        pl.semaphore_signal(barrier, inc=1, device_id=plane(source_of(0)), device_id_type=MESH)
    for step in range(1, 2 * NY):
        pl.semaphore_signal(barrier, inc=1, device_id=peer(step), device_id_type=MESH)
    loads[0].wait()
    pl.semaphore_wait(barrier, PEERS - 1 + 2 * NY - 1 + core)

    def pick(phase):
        for j in range(PEERS):
            picked[phase, j] = staged[phase][order[target(j)]]

    def send_in_plane(phase, piece):
        for j in range(PEERS):
            src, dst = picked.at[phase, j], pieces.at[piece, core, j]
            if j == 0:
                @pl.when(core == 0)
                def _():
                    pltpu.make_async_copy(src, dst, recv_plane.at[phase]).start()
                @pl.when(core == 1)
                def _():
                    copy_to(src, dst, self_sem.at[phase], recv_plane.at[phase], plane(target(j))).start()
            else:
                copy_to(src, dst, send_plane.at[phase], recv_plane.at[phase], plane(target(j))).start()

    def sent_in_plane(phase):
        most = picked.at[phase, pl.ds(1, PEERS - 1)]
        pltpu.make_async_copy(most, most, send_plane.at[phase]).wait()
        @pl.when(core == 1)
        def _():
            one = picked.at[phase, 0]
            pltpu.make_async_copy(one, one, self_sem.at[phase]).wait()

    def finish(piece, side, sem):
        part = pieces.at[piece, side]
        pltpu.make_async_copy(part, part, sem).wait()

    def to_ring(way, where):
        part = pieces.at[y, core]
        copy_to(part, part, send_ring.at[way], recv_ring.at[way], column(where, core)).start()

    def to_other(kind, piece):
        part = pieces.at[piece, core]
        copy_to(part, part, send_core.at[kind], recv_core.at[kind], column(y, other)).start()

    pick(0)
    send_in_plane(0, y)
    loads[1].wait()
    pick(1)
    loads[2].wait()
    chosen = order[lax.axis_index("pair")]
    prepare_left(lambda member: held[times[0, chosen], 0, member], columns, phases, 0, sink_left)
    prepare_left(lambda member: held[times[1, chosen], 0, member], columns, phases, 1, source_left)

    finish(y, core, recv_plane.at[0])
    to_ring(0, up)
    to_ring(1, down)
    send_in_plane(1, far)
    to_other(0, y)
    finish(y, other, recv_core.at[0])
    finish(down, core, recv_ring.at[0])
    to_other(1, down)
    finish(up, core, recv_ring.at[1])
    to_other(2, up)
    finish(far, core, recv_plane.at[1])
    to_other(3, far)
    finish(down, other, recv_core.at[1])
    finish(up, other, recv_core.at[2])
    finish(far, other, recv_core.at[3])

    gather_rows(pieces, block, x, z)
    sides(block, sink_left, source_left, sink, source)
    real, imaginary = slot_value(columns, sink, source, flipped)

    row = lax.broadcasted_iota(jnp.int32, (8, 128), 0)
    lane = lax.broadcasted_iota(jnp.int32, (8, 128), 1)
    both = jnp.where(row == 0, real, jnp.where(row == 1, imaginary, 0.0))
    votes[mom] = jnp.where(lane == group[0], both, 0.0)
    for step in range(1, 2 * NY):
        copy_to(votes.at[mom], votes.at[mom], send_vote.at[step], recv_vote.at[step], peer(step)).start()

    sent_in_plane(0)
    sent_in_plane(1)
    for way in range(2):
        finish(y, core, send_ring.at[way])
    for kind, piece in enumerate((y, down, up, far)):
        finish(piece, core, send_core.at[kind])
    for step in range(1, 2 * NY):
        sender = (mom + 2 * NY - step) % (2 * NY)
        pltpu.make_async_copy(votes.at[sender], votes.at[sender], recv_vote.at[step]).wait()
    total = votes[0]
    for each in range(1, 2 * NY):
        total = total + votes[each]
    out[0] = total[0:1, :GROUPS]
    out[1] = total[1:2, :GROUPS]
    for step in range(1, 2 * NY):
        pltpu.make_async_copy(votes.at[mom], votes.at[mom], send_vote.at[step]).wait()


def per_device(peramb, elementals, pair_times, pair_order, class_group, gamma_columns, gamma_phases):
    smem = pl.BlockSpec(memory_space=pltpu.SMEM)
    anywhere = pl.BlockSpec(memory_space=pl.ANY)
    dma = pltpu.SemaphoreType.DMA
    return pl.pallas_call(
        correlator_kernel,
        out_shape=jax.ShapeDtypeStruct((2, 1, GROUPS), F32),
        in_specs=[smem] * 5 + [anywhere] * 2,
        out_specs=pl.BlockSpec(memory_space=pltpu.VMEM),
        scratch_shapes=[
            pltpu.VMEM((NX * NZ, ROWS, PIECE), BF16),
            pltpu.VMEM((NX * NZ, ROWS, PIECE), BF16),
            pltpu.VMEM((2, PEERS, ROWS, PIECE), BF16),
            pltpu.VMEM((NY, 2, PEERS, ROWS, PIECE), BF16),
            pltpu.VMEM(elementals.shape, BF16),
            pltpu.VMEM((FULL, 2 * FULL), BF16),
            pltpu.VMEM((SPINS, 2, FULL, 256), BF16),
            pltpu.VMEM((SPINS, 2, FULL, 256), BF16),
            pltpu.VMEM((2, SPINS, VECTORS, 3 * FULL), BF16),
            pltpu.VMEM((2, SPINS, VECTORS, 3 * FULL), BF16),
            pltpu.VMEM((2, FULL, FULL), F32),
            pltpu.VMEM((2 * NY, 8, 128), F32),
            dma((3,)),
            dma((2,)),
            dma((2,)),
            dma((2,)),
            dma((2,)),
            dma((2,)),
            dma((4,)),
            dma((4,)),
            dma((2 * NY,)),
            dma((2 * NY,)),
        ],
        compiler_params=pltpu.CompilerParams(
            collective_id=0, has_side_effects=True, vmem_limit_bytes=60 * 1024 * 1024
        ),
        cost_estimate=pl.CostEstimate(flops=11_000_000_000, bytes_accessed=8_000_000, transcendentals=0),
        name="correlator",
    )(pair_order, pair_times.T, gamma_columns, gamma_phases, class_group, peramb, elementals)


def solution(mesh):
    placed = (P(None, "pair", None), P(None, "mom", None, None, None), P(), P(), P("mom"), P(), P())
    return jax.shard_map(
        per_device, mesh=mesh, in_specs=placed, out_specs=P(None, "pair", None), check_vma=False
    )
```

```python
import jax
import jax.numpy as jnp
from jax import lax
from jax.experimental import pallas as pl
from jax.experimental.pallas import tpu as pltpu
from jax.sharding import PartitionSpec as P

MESH = pl.DeviceIdType.MESH
F32 = jnp.float32
BF16 = jnp.bfloat16

NX, NZ, NY = 4, 8, 4
GROUPS = 8
SPINS = 4
VECTORS = 192
FULL = SPINS * VECTORS
ROWS = 24
PIECE = 384
PEERS = 16
STEPS = 4
EACH = PEERS // STEPS


def place():
    pair = lax.axis_index("pair")
    mom = lax.axis_index("mom")
    return pair // NZ, pair % NZ, mom // 2, mom % 2


def plane(pair):
    return {"pair": pair, "mom": lax.axis_index("mom")}


def column(y, core):
    return {"pair": lax.axis_index("pair"), "mom": y * 2 + core}


def copy_to(src, dst, send, recv, device):
    return pltpu.make_async_remote_copy(
        src_ref=src, dst_ref=dst, send_sem=send, recv_sem=recv, device_id=device, device_id_type=MESH
    )


def phase_parts(phase):
    real = jnp.where(phase == 0, 1.0, jnp.where(phase == 2, -1.0, 0.0)).astype(F32)
    imaginary = jnp.where(phase == 1, 1.0, jnp.where(phase == 3, -1.0, 0.0)).astype(F32)
    return real, imaginary


def spin_phases(columns, phases, side):
    found = []
    for spin in range(SPINS):
        real = jnp.float32(0.0)
        imaginary = jnp.float32(0.0)
        for row in range(SPINS):
            one, two = phase_parts(phases[side, row])
            chirality = 1.0 if (row if side == 0 else spin) < SPINS // 2 else -1.0
            here = jnp.where(columns[side, row] == spin, chirality, 0.0).astype(F32)
            real += here * one
            imaginary += here * two
        found.append((real, imaginary))
    return found


def padded_elements(tile):
    first = tile[:, :256].astype(F32)
    second = tile[:, 128:].astype(F32)
    lane = lax.broadcasted_iota(jnp.int32, first.shape, 1)
    real_low = jnp.where(lane < VECTORS, first, 0.0)
    imaginary_high = jnp.where(lane >= 64, second, 0.0)
    real_high = pltpu.roll(real_low, 64, 1)
    imaginary_low = pltpu.roll(imaginary_high, VECTORS, 1)
    return (real_low, imaginary_low), (real_high, imaginary_high)


def prepare_left(elements, columns, phases, side, left):
    turns = spin_phases(columns, phases, side)
    for member in range(2):
        padded = padded_elements(elements(member if side == 0 else 1 - member))
        for spin in range(SPINS):
            real, imaginary = padded[spin % 2]
            one, two = turns[spin]
            turned_real = one * real - two * imaginary
            turned_imaginary = one * imaginary + two * real
            base = member * 2 * VECTORS
            upper, lower = pl.ds(base, VECTORS), pl.ds(base + VECTORS, VECTORS)
            left[spin, 0, upper, :] = turned_real.astype(BF16)
            left[spin, 0, lower, :] = turned_imaginary.astype(BF16)
            if side == 0:
                left[spin, 1, upper, :] = (-turned_imaginary).astype(BF16)
                left[spin, 1, lower, :] = turned_real.astype(BF16)
            else:
                left[spin, 1, upper, :] = turned_imaginary.astype(BF16)
                left[spin, 1, lower, :] = (-turned_real).astype(BF16)


def gather_rows(pieces, block, x, z, piece):
    def position(s):
        dx, dz = (x + NX - s // NZ) % NX, (z + NZ - s % NZ) % NZ
        return dz % 2, dx * 4 + dz // 2

    def step(i, carry):
        one, two = position(2 * i), position(2 * i + 1)
        a = pieces[piece, one[0], one[1]].astype(F32)
        b = pieces[piece, two[0], two[1]].astype(F32)
        rows = pl.ds(pl.multiple_of(i * 2 * ROWS, 16), 2 * ROWS)
        block[rows, pl.ds(pl.multiple_of(piece * PIECE, 128), PIECE)] = jnp.concatenate([a, b], axis=0).astype(BF16)
        return carry

    lax.fori_loop(0, NX * NZ // 2, step, 0)


def product(left, right, dims):
    return lax.dot_general(left, right, (dims, ((), ())), preferred_element_type=F32)


def triple(real, imaginary, sign):
    real, imaginary = real.astype(BF16), imaginary.astype(BF16)
    one, two = real.astype(F32), imaginary.astype(F32)
    return real, imaginary, (one + two).astype(BF16), None if sign == 0 else (two - one).astype(BF16)


def lanes(start, width):
    return pl.ds(pl.multiple_of(start, 128), width)


def sink_part(block, sink_left, spin, step, part, piece):
    here = block[:, lanes(piece * PIECE + step * 128, 256)]
    return product(sink_left[spin, part], here, ((1,), (1,)))


def source_part(block, source_left, spin, part, piece):
    start = (spin // 2) * PIECE + (spin % 2) * 128
    here = block[start:start + 256, lanes(piece * PIECE, PIECE)]
    return product(source_left[spin, part], here, ((1,), (0,)))


def member_parts(turned, member):
    base = member * 2 * VECTORS
    return turned[base:base + VECTORS], turned[base + VECTORS:base + 2 * VECTORS]


def put_sink(sink, turned, spin):
    for member in range(2):
        real, imaginary, both, _ = triple(*member_parts(turned, member), 0)
        sink[member, spin, :, :FULL] = both
        sink[member, spin, :, FULL:2 * FULL] = real
        sink[member, spin, :, 2 * FULL:] = imaginary


def put_source(source, turned, spin, half):
    for member in range(2):
        real, _, both, less = triple(*member_parts(turned, member), 1)
        for place_of, value in enumerate((real, less, both)):
            source[member, spin, :, lanes(place_of * FULL + half * PIECE, PIECE)] = value


def begin_sides(block, sink_left, source_left, sink_sum, source_sum, half, part, piece):
    for step in range(2):
        sink_sum[step] = sink_part(block, sink_left, 2 * half + step, step, part, piece)
    for spin in range(SPINS):
        source_sum[spin] = source_part(block, source_left, spin, part, piece)


def end_sides(block, sink_left, source_left, sink_sum, source_sum, sink, source, half, part, piece):
    for step in range(2):
        spin = 2 * half + step
        put_sink(sink, sink_sum[step] + sink_part(block, sink_left, spin, step, part, piece), spin)
    for spin in range(SPINS):
        put_source(source, source_sum[spin] + source_part(block, source_left, spin, part, piece), spin, half)


def whole_sides(block, sink_left, source_left, sink, source, half):
    for step in range(2):
        spin = 2 * half + step
        turned = sink_part(block, sink_left, spin, step, 0, half)
        put_sink(sink, turned + sink_part(block, sink_left, spin, step, 1, half + 2), spin)
    for spin in range(SPINS):
        turned = source_part(block, source_left, spin, 0, half)
        put_source(source, turned + source_part(block, source_left, spin, 1, half + 2), spin, half)


WIDTH = 256


def meson_columns(columns, sink, source, member, n):
    found = []
    for part in range(3):
        left = jnp.concatenate(
            [sink[member, columns[0, spin], :, part * FULL:(part + 1) * FULL] for spin in range(SPINS)], axis=0
        )
        start = part * FULL + n * WIDTH
        right = jnp.concatenate(
            [source[member, columns[1, spin], :, start:start + WIDTH] for spin in range(SPINS)], axis=0
        )
        found.append(product(left, right, ((1,), (0,))))
    return found[0] - found[2], found[0] + found[1]


def folded(tile):
    return jnp.sum(tile.reshape(-1, 8, tile.shape[1]), axis=0)


def slot_value(columns, sink, source, flipped):
    eye = (
        lax.broadcasted_iota(jnp.int32, (WIDTH, WIDTH), 0) == lax.broadcasted_iota(jnp.int32, (WIDTH, WIDTH), 1)
    )
    zero = jnp.zeros((8, WIDTH), F32)
    traces = [[zero, zero], [zero, zero]]
    box_real = box_imaginary = zero
    for member in (1, 0):
        for n in range(FULL // WIDTH):
            at = slice(n * WIDTH, (n + 1) * WIDTH)
            parts = meson_columns(columns, sink, source, member, n)
            for part in range(2):
                traces[member][part] += folded(jnp.where(eye, parts[part][at], 0.0))
            if member == 1:
                for part in range(2):
                    flipped[part, at, :] = parts[part].T
            else:
                real, imaginary = parts
                box_real += folded(real * flipped[0, :, at] - imaginary * flipped[1, :, at])
                box_imaginary += folded(real * flipped[1, :, at] + imaginary * flipped[0, :, at])
    one_real, one_imaginary = (jnp.sum(part) for part in traces[0])
    two_real, two_imaginary = (jnp.sum(part) for part in traces[1])
    direct_real = one_real * two_real - one_imaginary * two_imaginary
    direct_imaginary = one_real * two_imaginary + one_imaginary * two_real
    return (direct_real - jnp.sum(box_real)) * 0.0625, (direct_imaginary - jnp.sum(box_imaginary)) * 0.0625


def correlator_kernel(
    order, times, columns, phases, group, peramb, elementals, out, staged_own, staged_far, picked, pieces, held, block,
    sink_left, source_left, sink, source, sink_sum, source_sum, flipped, votes, load_sem, self_sem, send_plane, recv_plane, send_ring,
    recv_ring, send_core, recv_core, send_vote, recv_vote,
):
    x, z, y, core = place()
    mom = lax.axis_index("mom")
    up, down, far = (y + 1) % NY, (y + NY - 1) % NY, (y + 2) % NY
    other = 1 - core

    def target(j):
        dx, dz = j // 4, 2 * (j % 4) + core
        return ((x + dx) % NX) * NZ + (z + dz) % NZ

    def source_of(j):
        dx, dz = j // 4, 2 * (j % 4) + core
        return ((x + NX - dx) % NX) * NZ + (z + NZ - dz) % NZ

    def peer(step):
        return {"pair": lax.axis_index("pair"), "mom": (mom + step) % (2 * NY)}

    staged = (staged_own, staged_far)
    loads = []
    for phase, piece in enumerate((y, far)):
        at = pl.ds(pl.multiple_of(piece * PIECE, 128), PIECE)
        loads.append(pltpu.make_async_copy(peramb.at[:, :, at], staged[phase], load_sem.at[phase]))
    loads.append(pltpu.make_async_copy(elementals, held, load_sem.at[2]))
    for load in loads:
        load.start()

    barrier = pltpu.get_barrier_semaphore()
    for j in range(1, PEERS):
        pl.semaphore_signal(barrier, inc=1, device_id=plane(source_of(j)), device_id_type=MESH)
    @pl.when(core == 1)
    def _():
        pl.semaphore_signal(barrier, inc=1, device_id=plane(source_of(0)), device_id_type=MESH)
    for step in range(1, 2 * NY):
        pl.semaphore_signal(barrier, inc=1, device_id=peer(step), device_id_type=MESH)
    def pick(phase):
        for j in range(PEERS):
            picked[phase, j] = staged[phase][order[target(j)]]

    def send_in_plane(phase, piece, g):
        for j in range(g * EACH, (g + 1) * EACH):
            src, dst = picked.at[phase, j], pieces.at[piece, core, j]
            sem = recv_plane.at[phase, g]
            if j == 0:
                @pl.when(core == 0)
                def _():
                    pltpu.make_async_copy(src, dst, sem).start()
                @pl.when(core == 1)
                def _():
                    copy_to(src, dst, self_sem.at[phase], sem, plane(target(j))).start()
            else:
                copy_to(src, dst, send_plane.at[phase], sem, plane(target(j))).start()

    def sent_in_plane(phase):
        most = picked.at[phase, pl.ds(1, PEERS - 1)]
        pltpu.make_async_copy(most, most, send_plane.at[phase]).wait()
        @pl.when(core == 1)
        def _():
            one = picked.at[phase, 0]
            pltpu.make_async_copy(one, one, self_sem.at[phase]).wait()

    def part(piece, side, g):
        return pieces.at[piece, side, pl.ds(g * EACH, EACH)]

    def finish(piece, side, sem, g):
        here = part(piece, side, g)
        pltpu.make_async_copy(here, here, sem).wait()

    def to_ring(way, where, g):
        here = part(y, core, g)
        copy_to(here, here, send_ring.at[way, g], recv_ring.at[way, g], column(where, core)).start()

    def to_other(kind, piece, g):
        here = part(piece, core, g)
        copy_to(here, here, send_core.at[kind, g], recv_core.at[kind, g], column(y, other)).start()

    loads[0].wait()
    pick(0)
    pl.semaphore_wait(barrier, PEERS - 1 + 2 * NY - 1 + core)
    for g in range(STEPS):
        send_in_plane(0, y, g)
    loads[1].wait()
    pick(1)
    for g in range(STEPS):
        send_in_plane(1, far, g)
    loads[2].wait()
    chosen = order[lax.axis_index("pair")]
    prepare_left(lambda member: held[times[0, chosen], 0, member], columns, phases, 0, sink_left)
    prepare_left(lambda member: held[times[1, chosen], 0, member], columns, phases, 1, source_left)

    for g in range(STEPS):
        finish(y, core, recv_plane.at[0, g], g)
        to_ring(0, up, g)
        to_ring(1, down, g)
        to_other(0, y, g)
    half, part_of = y % 2, y // 2
    for g in range(STEPS):
        finish(y, other, recv_core.at[0, g], g)
    gather_rows(pieces, block, x, z, y)
    begin_sides(block, sink_left, source_left, sink_sum, source_sum, half, part_of, y)

    for g in range(STEPS):
        finish(down, core, recv_ring.at[0, g], g)
        to_other(1, down, g)
        finish(up, core, recv_ring.at[1, g], g)
        to_other(2, up, g)
    for g in range(STEPS):
        finish(far, core, recv_plane.at[1, g], g)
        to_other(3, far, g)
    for g in range(STEPS):
        finish(down, other, recv_core.at[1, g], g)
        finish(up, other, recv_core.at[2, g], g)
    gather_rows(pieces, block, x, z, down)
    gather_rows(pieces, block, x, z, up)
    whole_sides(block, sink_left, source_left, sink, source, 1 - half)

    for g in range(STEPS):
        finish(far, other, recv_core.at[3, g], g)
    gather_rows(pieces, block, x, z, far)
    end_sides(block, sink_left, source_left, sink_sum, source_sum, sink, source, half, 1 - part_of, far)

    real, imaginary = slot_value(columns, sink, source, flipped)

    row = lax.broadcasted_iota(jnp.int32, (8, 128), 0)
    lane = lax.broadcasted_iota(jnp.int32, (8, 128), 1)
    both = jnp.where(row == 0, real, jnp.where(row == 1, imaginary, 0.0))
    votes[mom] = jnp.where(lane == group[0], both, 0.0)
    for step in range(1, 2 * NY):
        copy_to(votes.at[mom], votes.at[mom], send_vote.at[step], recv_vote.at[step], peer(step)).start()

    sent_in_plane(0)
    sent_in_plane(1)
    for g in range(STEPS):
        for way in range(2):
            finish(y, core, send_ring.at[way, g], g)
        for kind, piece in enumerate((y, down, up, far)):
            finish(piece, core, send_core.at[kind, g], g)
    for step in range(1, 2 * NY):
        sender = (mom + 2 * NY - step) % (2 * NY)
        pltpu.make_async_copy(votes.at[sender], votes.at[sender], recv_vote.at[step]).wait()
    total = votes[0]
    for each in range(1, 2 * NY):
        total = total + votes[each]
    out[...] = total
    for step in range(1, 2 * NY):
        pltpu.make_async_copy(votes.at[mom], votes.at[mom], send_vote.at[step]).wait()


def per_device(peramb, elementals, pair_times, pair_order, class_group, gamma_columns, gamma_phases):
    smem = pl.BlockSpec(memory_space=pltpu.SMEM)
    anywhere = pl.BlockSpec(memory_space=pl.ANY)
    dma = pltpu.SemaphoreType.DMA
    found = pl.pallas_call(
        correlator_kernel,
        out_shape=jax.ShapeDtypeStruct((8, 128), F32),
        in_specs=[smem] * 5 + [anywhere] * 2,
        out_specs=pl.BlockSpec(memory_space=pltpu.VMEM),
        scratch_shapes=[
            pltpu.VMEM((NX * NZ, ROWS, PIECE), BF16),
            pltpu.VMEM((NX * NZ, ROWS, PIECE), BF16),
            pltpu.VMEM((2, PEERS, ROWS, PIECE), BF16),
            pltpu.VMEM((NY, 2, PEERS, ROWS, PIECE), BF16),
            pltpu.VMEM(elementals.shape, BF16),
            pltpu.VMEM((FULL, 2 * FULL), BF16),
            pltpu.VMEM((SPINS, 2, FULL, 256), BF16),
            pltpu.VMEM((SPINS, 2, FULL, 256), BF16),
            pltpu.VMEM((2, SPINS, VECTORS, 3 * FULL), BF16),
            pltpu.VMEM((2, SPINS, VECTORS, 3 * FULL), BF16),
            pltpu.VMEM((2, FULL, FULL), F32),
            pltpu.VMEM((SPINS, FULL, PIECE), F32),
            pltpu.VMEM((2, FULL, FULL), F32),
            pltpu.VMEM((2 * NY, 8, 128), F32),
            dma((3,)),
            dma((2,)),
            dma((2,)),
            dma((2, STEPS)),
            dma((2, STEPS)),
            dma((2, STEPS)),
            dma((4, STEPS)),
            dma((4, STEPS)),
            dma((2 * NY,)),
            dma((2 * NY,)),
        ],
        compiler_params=pltpu.CompilerParams(
            collective_id=0, has_side_effects=True, vmem_limit_bytes=60 * 1024 * 1024
        ),
        cost_estimate=pl.CostEstimate(flops=11_000_000_000, bytes_accessed=8_000_000, transcendentals=0),
        name="correlator",
    )(pair_order, pair_times.T, gamma_columns, gamma_phases, class_group, peramb, elementals)
    return found[:2, :GROUPS].reshape(2, 1, GROUPS)


def solution(mesh):
    placed = (P(None, "pair", None), P(None, "mom", None, None, None), P(), P(), P("mom"), P(), P())
    return jax.shard_map(
        per_device, mesh=mesh, in_specs=placed, out_specs=P(None, "pair", None), check_vma=False
    )
```

```python
import jax
import jax.numpy as jnp
from jax import lax
from jax.experimental import pallas as pl
from jax.experimental.pallas import tpu as pltpu
from jax.sharding import PartitionSpec as P

MESH = pl.DeviceIdType.MESH
F32 = jnp.float32
BF16 = jnp.bfloat16

NX, NZ, NY = 4, 8, 4
GROUPS = 8
SPINS = 4
VECTORS = 192
FULL = SPINS * VECTORS
ROWS = 24
PIECE = 384
PEERS = 16
STEPS = 4
EACH = PEERS // STEPS
OFFSETS = (
    (0, 0), (0, 3), (1, 0), (3, 0), (0, 1), (1, 3), (3, 3), (2, 0),
    (0, 2), (1, 1), (3, 1), (2, 3), (1, 2), (3, 2), (2, 1), (2, 2),
)


def place():
    pair = lax.axis_index("pair")
    mom = lax.axis_index("mom")
    return pair // NZ, pair % NZ, mom // 2, mom % 2


def plane(pair):
    return {"pair": pair, "mom": lax.axis_index("mom")}


def column(y, core):
    return {"pair": lax.axis_index("pair"), "mom": y * 2 + core}


def copy_to(src, dst, send, recv, device):
    return pltpu.make_async_remote_copy(
        src_ref=src, dst_ref=dst, send_sem=send, recv_sem=recv, device_id=device, device_id_type=MESH
    )


def phase_parts(phase):
    real = jnp.where(phase == 0, 1.0, jnp.where(phase == 2, -1.0, 0.0)).astype(F32)
    imaginary = jnp.where(phase == 1, 1.0, jnp.where(phase == 3, -1.0, 0.0)).astype(F32)
    return real, imaginary


def spin_phases(columns, phases, side):
    found = []
    for spin in range(SPINS):
        real = jnp.float32(0.0)
        imaginary = jnp.float32(0.0)
        for row in range(SPINS):
            one, two = phase_parts(phases[side, row])
            chirality = 1.0 if (row if side == 0 else spin) < SPINS // 2 else -1.0
            here = jnp.where(columns[side, row] == spin, chirality, 0.0).astype(F32)
            real += here * one
            imaginary += here * two
        found.append((real, imaginary))
    return found


def padded_elements(tile):
    first = tile[:, :256].astype(F32)
    second = tile[:, 128:].astype(F32)
    lane = lax.broadcasted_iota(jnp.int32, first.shape, 1)
    real_low = jnp.where(lane < VECTORS, first, 0.0)
    imaginary_high = jnp.where(lane >= 64, second, 0.0)
    real_high = pltpu.roll(real_low, 64, 1)
    imaginary_low = pltpu.roll(imaginary_high, VECTORS, 1)
    return (real_low, imaginary_low), (real_high, imaginary_high)


def prepare_left(elements, columns, phases, side, left):
    turns = spin_phases(columns, phases, side)
    for member in range(2):
        padded = padded_elements(elements(member if side == 0 else 1 - member))
        for spin in range(SPINS):
            real, imaginary = padded[spin % 2]
            one, two = turns[spin]
            turned_real = one * real - two * imaginary
            turned_imaginary = one * imaginary + two * real
            base = member * 2 * VECTORS
            upper, lower = pl.ds(base, VECTORS), pl.ds(base + VECTORS, VECTORS)
            left[spin, 0, upper, :] = turned_real.astype(BF16)
            left[spin, 0, lower, :] = turned_imaginary.astype(BF16)
            if side == 0:
                left[spin, 1, upper, :] = (-turned_imaginary).astype(BF16)
                left[spin, 1, lower, :] = turned_real.astype(BF16)
            else:
                left[spin, 1, upper, :] = turned_imaginary.astype(BF16)
                left[spin, 1, lower, :] = (-turned_real).astype(BF16)


def gather_rows(pieces, block, x, z, piece):
    odd = z % 2
    for dx in range(NX):
        for v in range(4):
            first = OFFSETS.index((dx, v))
            second = jnp.where(odd == 1, first, OFFSETS.index((dx, (v + 3) % 4)))
            pair = ((x + NX - dx) % NX) * NZ + (z + NZ - 2 * v - odd) % NZ
            a = pieces[piece, odd, first].astype(F32)
            b = pieces[piece, 1 - odd, second].astype(F32)
            rows = pl.ds(pl.multiple_of(pair * ROWS, 16), 2 * ROWS)
            block[rows, pl.ds(pl.multiple_of(piece * PIECE, 128), PIECE)] = jnp.concatenate([a, b], axis=0).astype(BF16)


def product(left, right, dims):
    return lax.dot_general(left, right, (dims, ((), ())), preferred_element_type=F32)


def triple(real, imaginary, sign):
    real, imaginary = real.astype(BF16), imaginary.astype(BF16)
    one, two = real.astype(F32), imaginary.astype(F32)
    return real, imaginary, (one + two).astype(BF16), None if sign == 0 else (two - one).astype(BF16)


def lanes(start, width):
    return pl.ds(pl.multiple_of(start, 128), width)


def sink_part(block, sink_left, spin, step, part, piece):
    here = block[:, lanes(piece * PIECE + step * 128, 256)]
    return product(sink_left[spin, part], here, ((1,), (1,)))


def member_parts(turned, member):
    base = member * 2 * VECTORS
    return turned[base:base + VECTORS], turned[base + VECTORS:base + 2 * VECTORS]


def put_sink(sink, turned, spin):
    for member in range(2):
        real, imaginary, both, _ = triple(*member_parts(turned, member), 0)
        sink[member, spin, :, :FULL] = both
        sink[member, spin, :, FULL:2 * FULL] = real
        sink[member, spin, :, 2 * FULL:] = imaginary


def begin_sink(block, sink_left, sink_sum, half, part, piece):
    for step in range(2):
        sink_sum[step] = sink_part(block, sink_left, 2 * half + step, step, part, piece)


def end_sink(block, sink_left, sink_sum, sink, half, part, piece):
    for step in range(2):
        spin = 2 * half + step
        put_sink(sink, sink_sum[step] + sink_part(block, sink_left, spin, step, part, piece), spin)


def whole_sink(block, sink_left, sink, half):
    for step in range(2):
        spin = 2 * half + step
        turned = sink_part(block, sink_left, spin, step, 0, half)
        put_sink(sink, turned + sink_part(block, sink_left, spin, step, 1, half + 2), spin)


def whole_source(block, source_left, source):
    for spin in range(SPINS):
        start = (spin // 2) * PIECE + (spin % 2) * 128
        turned = product(source_left[spin, 0], block[start:start + 256, :FULL], ((1,), (0,)))
        turned += product(source_left[spin, 1], block[start:start + 256, FULL:], ((1,), (0,)))
        for member in range(2):
            real, _, both, less = triple(*member_parts(turned, member), 1)
            source[member, spin, :, :FULL] = real
            source[member, spin, :, FULL:2 * FULL] = less
            source[member, spin, :, 2 * FULL:] = both


WIDTH = 256


def meson_columns(columns, sink, source, member, n):
    found = []
    for part in range(3):
        left = jnp.concatenate(
            [sink[member, columns[0, spin], :, part * FULL:(part + 1) * FULL] for spin in range(SPINS)], axis=0
        )
        start = part * FULL + n * WIDTH
        right = jnp.concatenate(
            [source[member, columns[1, spin], :, start:start + WIDTH] for spin in range(SPINS)], axis=0
        )
        found.append(product(left, right, ((1,), (0,))))
    return found[0] - found[2], found[0] + found[1]


def folded(tile):
    return jnp.sum(tile.reshape(-1, 8, tile.shape[1]), axis=0)


def slot_value(columns, sink, source, flipped):
    eye = (
        lax.broadcasted_iota(jnp.int32, (WIDTH, WIDTH), 0) == lax.broadcasted_iota(jnp.int32, (WIDTH, WIDTH), 1)
    )
    zero = jnp.zeros((8, WIDTH), F32)
    traces = [[zero, zero], [zero, zero]]
    box_real = box_imaginary = zero
    for member in (1, 0):
        for n in range(FULL // WIDTH):
            at = slice(n * WIDTH, (n + 1) * WIDTH)
            parts = meson_columns(columns, sink, source, member, n)
            for part in range(2):
                traces[member][part] += folded(jnp.where(eye, parts[part][at], 0.0))
            if member == 1:
                for part in range(2):
                    flipped[part, at, :] = parts[part].T
            else:
                real, imaginary = parts
                box_real += folded(real * flipped[0, :, at] - imaginary * flipped[1, :, at])
                box_imaginary += folded(real * flipped[1, :, at] + imaginary * flipped[0, :, at])
    one_real, one_imaginary = (jnp.sum(part) for part in traces[0])
    two_real, two_imaginary = (jnp.sum(part) for part in traces[1])
    direct_real = one_real * two_real - one_imaginary * two_imaginary
    direct_imaginary = one_real * two_imaginary + one_imaginary * two_real
    return (direct_real - jnp.sum(box_real)) * 0.0625, (direct_imaginary - jnp.sum(box_imaginary)) * 0.0625


def correlator_kernel(
    order, times, columns, phases, group, peramb, elementals, out, staged_own, staged_far, picked, pieces, held, block,
    sink_left, source_left, sink, source, sink_sum, flipped, votes, load_sem, self_sem, send_plane, recv_plane, send_ring,
    recv_ring, send_core, recv_core, send_vote, recv_vote,
):
    x, z, y, core = place()
    mom = lax.axis_index("mom")
    up, down, far = (y + 1) % NY, (y + NY - 1) % NY, (y + 2) % NY
    other = 1 - core

    def target(j):
        dx, dz = OFFSETS[j][0], 2 * OFFSETS[j][1] + core
        return ((x + dx) % NX) * NZ + (z + dz) % NZ

    def source_of(j):
        dx, dz = OFFSETS[j][0], 2 * OFFSETS[j][1] + core
        return ((x + NX - dx) % NX) * NZ + (z + NZ - dz) % NZ

    def peer(step):
        return {"pair": lax.axis_index("pair"), "mom": (mom + step) % (2 * NY)}

    staged = (staged_own, staged_far)
    loads = []
    for phase, piece in enumerate((y, far)):
        at = pl.ds(pl.multiple_of(piece * PIECE, 128), PIECE)
        loads.append(pltpu.make_async_copy(peramb.at[:, :, at], staged[phase], load_sem.at[phase]))
    loads.append(pltpu.make_async_copy(elementals, held, load_sem.at[2]))
    for load in loads:
        load.start()

    barrier = pltpu.get_barrier_semaphore()
    for j in range(1, PEERS):
        pl.semaphore_signal(barrier, inc=1, device_id=plane(source_of(j)), device_id_type=MESH)
    @pl.when(core == 1)
    def _():
        pl.semaphore_signal(barrier, inc=1, device_id=plane(source_of(0)), device_id_type=MESH)
    for step in range(1, 2 * NY):
        pl.semaphore_signal(barrier, inc=1, device_id=peer(step), device_id_type=MESH)
    def pick(phase):
        for j in range(PEERS):
            picked[phase, j] = staged[phase][order[target(j)]]

    def send_in_plane(phase, piece, g):
        for j in range(g * EACH, (g + 1) * EACH):
            src, dst = picked.at[phase, j], pieces.at[piece, core, j]
            sem = recv_plane.at[phase, g]
            if j == 0:
                @pl.when(core == 0)
                def _():
                    pltpu.make_async_copy(src, dst, sem).start()
                @pl.when(core == 1)
                def _():
                    copy_to(src, dst, self_sem.at[phase], sem, plane(target(j))).start()
            else:
                copy_to(src, dst, send_plane.at[phase], sem, plane(target(j))).start()

    def sent_in_plane(phase):
        most = picked.at[phase, pl.ds(1, PEERS - 1)]
        pltpu.make_async_copy(most, most, send_plane.at[phase]).wait()
        @pl.when(core == 1)
        def _():
            one = picked.at[phase, 0]
            pltpu.make_async_copy(one, one, self_sem.at[phase]).wait()

    def part(piece, side, g):
        return pieces.at[piece, side, pl.ds(g * EACH, EACH)]

    def finish(piece, side, sem, g):
        here = part(piece, side, g)
        pltpu.make_async_copy(here, here, sem).wait()

    def to_ring(way, where, g):
        here = part(y, core, g)
        copy_to(here, here, send_ring.at[way, g], recv_ring.at[way, g], column(where, core)).start()

    def to_other(kind, piece, g):
        here = part(piece, core, g)
        copy_to(here, here, send_core.at[kind, g], recv_core.at[kind, g], column(y, other)).start()

    loads[0].wait()
    pick(0)
    pl.semaphore_wait(barrier, PEERS - 1 + 2 * NY - 1 + core)
    for g in range(STEPS):
        send_in_plane(0, y, g)
    loads[1].wait()
    pick(1)
    for g in range(STEPS):
        send_in_plane(1, far, g)
    loads[2].wait()
    chosen = order[lax.axis_index("pair")]
    prepare_left(lambda member: held[times[0, chosen], 0, member], columns, phases, 0, sink_left)
    prepare_left(lambda member: held[times[1, chosen], 0, member], columns, phases, 1, source_left)

    for g in range(STEPS):
        finish(y, core, recv_plane.at[0, g], g)
        to_ring(0, up, g)
        to_ring(1, down, g)
        to_other(0, y, g)
    half, part_of = y % 2, y // 2
    for g in range(STEPS):
        finish(y, other, recv_core.at[0, g], g)
    gather_rows(pieces, block, x, z, y)
    begin_sink(block, sink_left, sink_sum, half, part_of, y)

    for g in range(STEPS):
        finish(down, core, recv_ring.at[0, g], g)
        to_other(1, down, g)
        finish(up, core, recv_ring.at[1, g], g)
        to_other(2, up, g)
    for g in range(STEPS):
        finish(far, core, recv_plane.at[1, g], g)
        to_other(3, far, g)
    for g in range(STEPS):
        finish(down, other, recv_core.at[1, g], g)
        finish(up, other, recv_core.at[2, g], g)
    gather_rows(pieces, block, x, z, down)
    gather_rows(pieces, block, x, z, up)
    whole_sink(block, sink_left, sink, 1 - half)

    for g in range(STEPS):
        finish(far, other, recv_core.at[3, g], g)
    gather_rows(pieces, block, x, z, far)
    end_sink(block, sink_left, sink_sum, sink, half, 1 - part_of, far)
    whole_source(block, source_left, source)

    real, imaginary = slot_value(columns, sink, source, flipped)

    row = lax.broadcasted_iota(jnp.int32, (8, 128), 0)
    lane = lax.broadcasted_iota(jnp.int32, (8, 128), 1)
    both = jnp.where(row == 0, real, jnp.where(row == 1, imaginary, 0.0))
    votes[mom] = jnp.where(lane == group[0], both, 0.0)
    for step in range(1, 2 * NY):
        copy_to(votes.at[mom], votes.at[mom], send_vote.at[step], recv_vote.at[step], peer(step)).start()

    sent_in_plane(0)
    sent_in_plane(1)
    for g in range(STEPS):
        for way in range(2):
            finish(y, core, send_ring.at[way, g], g)
        for kind, piece in enumerate((y, down, up, far)):
            finish(piece, core, send_core.at[kind, g], g)
    for step in range(1, 2 * NY):
        sender = (mom + 2 * NY - step) % (2 * NY)
        pltpu.make_async_copy(votes.at[sender], votes.at[sender], recv_vote.at[step]).wait()
    total = votes[0]
    for each in range(1, 2 * NY):
        total = total + votes[each]
    out[...] = total
    for step in range(1, 2 * NY):
        pltpu.make_async_copy(votes.at[mom], votes.at[mom], send_vote.at[step]).wait()


def per_device(peramb, elementals, pair_times, pair_order, class_group, gamma_columns, gamma_phases):
    smem = pl.BlockSpec(memory_space=pltpu.SMEM)
    anywhere = pl.BlockSpec(memory_space=pl.ANY)
    dma = pltpu.SemaphoreType.DMA
    found = pl.pallas_call(
        correlator_kernel,
        out_shape=jax.ShapeDtypeStruct((8, 128), F32),
        in_specs=[smem] * 5 + [anywhere] * 2,
        out_specs=pl.BlockSpec(memory_space=pltpu.VMEM),
        scratch_shapes=[
            pltpu.VMEM((NX * NZ, ROWS, PIECE), BF16),
            pltpu.VMEM((NX * NZ, ROWS, PIECE), BF16),
            pltpu.VMEM((2, PEERS, ROWS, PIECE), BF16),
            pltpu.VMEM((NY, 2, PEERS, ROWS, PIECE), BF16),
            pltpu.VMEM(elementals.shape, BF16),
            pltpu.VMEM((FULL, 2 * FULL), BF16),
            pltpu.VMEM((SPINS, 2, FULL, 256), BF16),
            pltpu.VMEM((SPINS, 2, FULL, 256), BF16),
            pltpu.VMEM((2, SPINS, VECTORS, 3 * FULL), BF16),
            pltpu.VMEM((2, SPINS, VECTORS, 3 * FULL), BF16),
            pltpu.VMEM((2, FULL, FULL), F32),
            pltpu.VMEM((2, FULL, FULL), F32),
            pltpu.VMEM((2 * NY, 8, 128), F32),
            dma((3,)),
            dma((2,)),
            dma((2,)),
            dma((2, STEPS)),
            dma((2, STEPS)),
            dma((2, STEPS)),
            dma((4, STEPS)),
            dma((4, STEPS)),
            dma((2 * NY,)),
            dma((2 * NY,)),
        ],
        compiler_params=pltpu.CompilerParams(
            collective_id=0, has_side_effects=True, vmem_limit_bytes=60 * 1024 * 1024
        ),
        cost_estimate=pl.CostEstimate(flops=11_000_000_000, bytes_accessed=8_000_000, transcendentals=0),
        name="correlator",
    )(pair_order, pair_times.T, gamma_columns, gamma_phases, class_group, peramb, elementals)
    return found[:2, :GROUPS].reshape(2, 1, GROUPS)


def solution(mesh):
    placed = (P(None, "pair", None), P(None, "mom", None, None, None), P(), P(), P("mom"), P(), P())
    return jax.shard_map(
        per_device, mesh=mesh, in_specs=placed, out_specs=P(None, "pair", None), check_vma=False
    )
```

```python
import jax
import jax.numpy as jnp
from jax import lax
from jax.experimental import pallas as pl
from jax.experimental.pallas import tpu as pltpu
from jax.sharding import PartitionSpec as P

MESH = pl.DeviceIdType.MESH
F32 = jnp.float32
BF16 = jnp.bfloat16

NX, NZ, NY = 4, 8, 4
GROUPS = 8
SPINS = 4
VECTORS = 192
FULL = SPINS * VECTORS
ROWS = 24
PIECE = 384
PEERS = 16
STEPS = 4
EACH = PEERS // STEPS
OFFSETS = (
    (0, 0), (0, 3), (1, 0), (3, 0), (0, 1), (1, 3), (3, 3), (2, 0),
    (0, 2), (1, 1), (3, 1), (2, 3), (1, 2), (3, 2), (2, 1), (2, 2),
)


def place():
    pair = lax.axis_index("pair")
    mom = lax.axis_index("mom")
    return pair // NZ, pair % NZ, mom // 2, mom % 2


def plane(pair):
    return {"pair": pair, "mom": lax.axis_index("mom")}


def column(y, core):
    return {"pair": lax.axis_index("pair"), "mom": y * 2 + core}


def copy_to(src, dst, send, recv, device):
    return pltpu.make_async_remote_copy(
        src_ref=src, dst_ref=dst, send_sem=send, recv_sem=recv, device_id=device, device_id_type=MESH
    )


def phase_parts(phase):
    real = jnp.where(phase == 0, 1.0, jnp.where(phase == 2, -1.0, 0.0)).astype(F32)
    imaginary = jnp.where(phase == 1, 1.0, jnp.where(phase == 3, -1.0, 0.0)).astype(F32)
    return real, imaginary


def spin_phases(columns, phases, side):
    found = []
    for spin in range(SPINS):
        real = jnp.float32(0.0)
        imaginary = jnp.float32(0.0)
        for row in range(SPINS):
            one, two = phase_parts(phases[side, row])
            chirality = 1.0 if (row if side == 0 else spin) < SPINS // 2 else -1.0
            here = jnp.where(columns[side, row] == spin, chirality, 0.0).astype(F32)
            real += here * one
            imaginary += here * two
        found.append((real, imaginary))
    return found


def padded_elements(tile):
    first = tile[:, :256].astype(F32)
    second = tile[:, 128:].astype(F32)
    lane = lax.broadcasted_iota(jnp.int32, first.shape, 1)
    real_low = jnp.where(lane < VECTORS, first, 0.0)
    imaginary_high = jnp.where(lane >= 64, second, 0.0)
    real_high = pltpu.roll(real_low, 64, 1)
    imaginary_low = pltpu.roll(imaginary_high, VECTORS, 1)
    return (real_low, imaginary_low), (real_high, imaginary_high)


def prepare_left(elements, columns, phases, side, left):
    turns = spin_phases(columns, phases, side)
    for member in range(2):
        padded = padded_elements(elements(member if side == 0 else 1 - member))
        for spin in range(SPINS):
            real, imaginary = padded[spin % 2]
            one, two = turns[spin]
            turned_real = one * real - two * imaginary
            turned_imaginary = one * imaginary + two * real
            base = member * 2 * VECTORS
            upper, lower = pl.ds(base, VECTORS), pl.ds(base + VECTORS, VECTORS)
            left[spin, 0, upper, :] = turned_real.astype(BF16)
            left[spin, 0, lower, :] = turned_imaginary.astype(BF16)
            if side == 0:
                left[spin, 1, upper, :] = (-turned_imaginary).astype(BF16)
                left[spin, 1, lower, :] = turned_real.astype(BF16)
            else:
                left[spin, 1, upper, :] = turned_imaginary.astype(BF16)
                left[spin, 1, lower, :] = (-turned_real).astype(BF16)


def gather_rows(pieces, block, x, z, piece):
    odd = z % 2
    for dx in range(NX):
        for v in range(4):
            first = OFFSETS.index((dx, v))
            second = jnp.where(odd == 1, first, OFFSETS.index((dx, (v + 3) % 4)))
            pair = ((x + NX - dx) % NX) * NZ + (z + NZ - 2 * v - odd) % NZ
            a = pieces[piece, odd, first].astype(F32)
            b = pieces[piece, 1 - odd, second].astype(F32)
            rows = pl.ds(pl.multiple_of(pair * ROWS, 16), 2 * ROWS)
            block[rows, pl.ds(pl.multiple_of(piece * PIECE, 128), PIECE)] = jnp.concatenate([a, b], axis=0).astype(BF16)


def product(left, right, dims):
    return lax.dot_general(left, right, (dims, ((), ())), preferred_element_type=F32)


def triple(real, imaginary, sign):
    real, imaginary = real.astype(BF16), imaginary.astype(BF16)
    one, two = real.astype(F32), imaginary.astype(F32)
    return real, imaginary, (one + two).astype(BF16), None if sign == 0 else (two - one).astype(BF16)


def lanes(start, width):
    return pl.ds(pl.multiple_of(start, 128), width)


def sink_part(block, sink_left, spin, step, part, piece):
    here = block[:, lanes(piece * PIECE + step * 128, 256)]
    return product(sink_left[spin, part], here, ((1,), (1,)))


def member_parts(turned, member):
    base = member * 2 * VECTORS
    return turned[base:base + VECTORS], turned[base + VECTORS:base + 2 * VECTORS]


def put_sink(sink, turned, spin):
    for member in range(2):
        real, imaginary, both, _ = triple(*member_parts(turned, member), 0)
        sink[member, spin, :, :FULL] = both
        sink[member, spin, :, FULL:2 * FULL] = real
        sink[member, spin, :, 2 * FULL:] = imaginary


def begin_sink(block, sink_left, sink_sum, half, part, piece):
    for step in range(2):
        sink_sum[step] = sink_part(block, sink_left, 2 * half + step, step, part, piece)


def end_sink(block, sink_left, sink_sum, sink, half, part, piece):
    for step in range(2):
        spin = 2 * half + step
        put_sink(sink, sink_sum[step] + sink_part(block, sink_left, spin, step, part, piece), spin)


def whole_sink(block, sink_left, sink, half):
    for step in range(2):
        spin = 2 * half + step
        turned = sink_part(block, sink_left, spin, step, 0, half)
        put_sink(sink, turned + sink_part(block, sink_left, spin, step, 1, half + 2), spin)


def whole_source(block, source_left, source):
    for spin in range(SPINS):
        start = (spin // 2) * PIECE + (spin % 2) * 128
        turned = product(source_left[spin, 0], block[start:start + 256, :FULL], ((1,), (0,)))
        turned += product(source_left[spin, 1], block[start:start + 256, FULL:], ((1,), (0,)))
        for member in range(2):
            real, _, both, less = triple(*member_parts(turned, member), 1)
            source[member, spin, :, :FULL] = real
            source[member, spin, :, FULL:2 * FULL] = less
            source[member, spin, :, 2 * FULL:] = both


WIDTH = 256


def meson_columns(columns, sink, source, member, n):
    found = []
    for part in range(3):
        left = jnp.concatenate(
            [sink[member, columns[0, spin], :, part * FULL:(part + 1) * FULL] for spin in range(SPINS)], axis=0
        )
        start = part * FULL + n * WIDTH
        right = jnp.concatenate(
            [source[member, columns[1, spin], :, start:start + WIDTH] for spin in range(SPINS)], axis=0
        )
        found.append(product(left, right, ((1,), (0,))))
    return found[0] - found[2], found[0] + found[1]


def folded(tile):
    return jnp.sum(tile.reshape(-1, 8, tile.shape[1]), axis=0)


def slot_value(columns, sink, source, flipped):
    eye = (
        lax.broadcasted_iota(jnp.int32, (WIDTH, WIDTH), 0) == lax.broadcasted_iota(jnp.int32, (WIDTH, WIDTH), 1)
    )
    zero = jnp.zeros((8, WIDTH), F32)
    traces = [[zero, zero], [zero, zero]]
    box_real = box_imaginary = zero
    for member in (1, 0):
        for n in range(FULL // WIDTH):
            at = slice(n * WIDTH, (n + 1) * WIDTH)
            parts = meson_columns(columns, sink, source, member, n)
            for part in range(2):
                traces[member][part] += folded(jnp.where(eye, parts[part][at], 0.0))
            if member == 1:
                for part in range(2):
                    flipped[part, at, :] = parts[part].T
            else:
                real, imaginary = parts
                box_real += folded(real * flipped[0, :, at] - imaginary * flipped[1, :, at])
                box_imaginary += folded(real * flipped[1, :, at] + imaginary * flipped[0, :, at])
    one_real, one_imaginary = (jnp.sum(part) for part in traces[0])
    two_real, two_imaginary = (jnp.sum(part) for part in traces[1])
    direct_real = one_real * two_real - one_imaginary * two_imaginary
    direct_imaginary = one_real * two_imaginary + one_imaginary * two_real
    return (direct_real - jnp.sum(box_real)) * 0.0625, (direct_imaginary - jnp.sum(box_imaginary)) * 0.0625


def correlator_kernel(
    order, times, columns, phases, group, peramb, elementals, out, staged_own, staged_far, picked, pieces, held, block,
    sink_left, source_left, sink, source, sink_sum, flipped, votes, load_sem, self_sem, send_plane, recv_plane, send_ring,
    recv_ring, send_core, recv_core, send_vote, recv_vote,
):
    x, z, y, core = place()
    mom = lax.axis_index("mom")
    up, down, far = (y + 1) % NY, (y + NY - 1) % NY, (y + 2) % NY
    other = 1 - core

    def target(j):
        dx, dz = OFFSETS[j][0], 2 * OFFSETS[j][1] + core
        return ((x + dx) % NX) * NZ + (z + dz) % NZ

    def source_of(j):
        dx, dz = OFFSETS[j][0], 2 * OFFSETS[j][1] + core
        return ((x + NX - dx) % NX) * NZ + (z + NZ - dz) % NZ

    def peer(step):
        return {"pair": lax.axis_index("pair"), "mom": (mom + step) % (2 * NY)}

    staged = (staged_own, staged_far)
    loads = []
    for phase, piece in enumerate((y, far)):
        at = pl.ds(pl.multiple_of(piece * PIECE, 128), PIECE)
        loads.append(pltpu.make_async_copy(peramb.at[:, :, at], staged[phase], load_sem.at[phase]))
    loads.append(pltpu.make_async_copy(elementals, held, load_sem.at[2]))
    for load in loads:
        load.start()

    barrier = pltpu.get_barrier_semaphore()
    for j in range(1, PEERS):
        pl.semaphore_signal(barrier, inc=1, device_id=plane(source_of(j)), device_id_type=MESH)
    @pl.when(core == 1)
    def _():
        pl.semaphore_signal(barrier, inc=1, device_id=plane(source_of(0)), device_id_type=MESH)
    for step in range(1, 2 * NY):
        pl.semaphore_signal(barrier, inc=1, device_id=peer(step), device_id_type=MESH)
    def pick(phase):
        for j in range(PEERS):
            picked[phase, j] = staged[phase][order[target(j)]]

    def send_in_plane(phase, piece, g):
        for j in range(g * EACH, (g + 1) * EACH):
            src, dst = picked.at[phase, j], pieces.at[piece, core, j]
            sem = recv_plane.at[phase, g]
            if j == 0:
                @pl.when(core == 0)
                def _():
                    pltpu.make_async_copy(src, dst, sem).start()
                @pl.when(core == 1)
                def _():
                    copy_to(src, dst, self_sem.at[phase], sem, plane(target(j))).start()
            else:
                copy_to(src, dst, send_plane.at[phase], sem, plane(target(j))).start()

    def sent_in_plane(phase):
        most = picked.at[phase, pl.ds(1, PEERS - 1)]
        pltpu.make_async_copy(most, most, send_plane.at[phase]).wait()
        @pl.when(core == 1)
        def _():
            one = picked.at[phase, 0]
            pltpu.make_async_copy(one, one, self_sem.at[phase]).wait()

    def part(piece, side, g):
        return pieces.at[piece, side, pl.ds(g * EACH, EACH)]

    def finish(piece, side, sem, g):
        here = part(piece, side, g)
        pltpu.make_async_copy(here, here, sem).wait()

    def to_ring(way, where, g):
        here = part(y, core, g)
        copy_to(here, here, send_ring.at[way, g], recv_ring.at[way, g], column(where, core)).start()

    def to_other(kind, piece, g):
        here = part(piece, core, g)
        copy_to(here, here, send_core.at[kind, g], recv_core.at[kind, g], column(y, other)).start()

    loads[0].wait()
    pick(0)
    pl.semaphore_wait(barrier, PEERS - 1 + 2 * NY - 1 + core)
    for g in range(STEPS):
        send_in_plane(0, y, g)
    loads[1].wait()
    pick(1)
    loads[2].wait()
    chosen = order[lax.axis_index("pair")]
    prepare_left(lambda member: held[times[0, chosen], 0, member], columns, phases, 0, sink_left)
    prepare_left(lambda member: held[times[1, chosen], 0, member], columns, phases, 1, source_left)

    for g in range(STEPS):
        finish(y, core, recv_plane.at[0, g], g)
        to_ring(0, up, g)
        to_ring(1, down, g)
        if g == 0:
            for later in range(STEPS):
                send_in_plane(1, far, later)
        to_other(0, y, g)
    half, part_of = y % 2, y // 2
    for g in range(STEPS):
        finish(y, other, recv_core.at[0, g], g)
    gather_rows(pieces, block, x, z, y)
    begin_sink(block, sink_left, sink_sum, half, part_of, y)

    for g in range(STEPS):
        finish(down, core, recv_ring.at[0, g], g)
        to_other(1, down, g)
        finish(up, core, recv_ring.at[1, g], g)
        to_other(2, up, g)
    for g in range(STEPS):
        finish(far, core, recv_plane.at[1, g], g)
        to_other(3, far, g)
    for g in range(STEPS):
        finish(down, other, recv_core.at[1, g], g)
        finish(up, other, recv_core.at[2, g], g)
    gather_rows(pieces, block, x, z, down)
    gather_rows(pieces, block, x, z, up)
    whole_sink(block, sink_left, sink, 1 - half)

    for g in range(STEPS):
        finish(far, other, recv_core.at[3, g], g)
    gather_rows(pieces, block, x, z, far)
    end_sink(block, sink_left, sink_sum, sink, half, 1 - part_of, far)
    whole_source(block, source_left, source)

    real, imaginary = slot_value(columns, sink, source, flipped)

    row = lax.broadcasted_iota(jnp.int32, (8, 128), 0)
    lane = lax.broadcasted_iota(jnp.int32, (8, 128), 1)
    both = jnp.where(row == 0, real, jnp.where(row == 1, imaginary, 0.0))
    votes[mom] = jnp.where(lane == group[0], both, 0.0)
    for step in range(1, 2 * NY):
        copy_to(votes.at[mom], votes.at[mom], send_vote.at[step], recv_vote.at[step], peer(step)).start()

    sent_in_plane(0)
    sent_in_plane(1)
    for g in range(STEPS):
        for way in range(2):
            finish(y, core, send_ring.at[way, g], g)
        for kind, piece in enumerate((y, down, up, far)):
            finish(piece, core, send_core.at[kind, g], g)
    for step in range(1, 2 * NY):
        sender = (mom + 2 * NY - step) % (2 * NY)
        pltpu.make_async_copy(votes.at[sender], votes.at[sender], recv_vote.at[step]).wait()
    total = votes[0]
    for each in range(1, 2 * NY):
        total = total + votes[each]
    out[...] = total
    for step in range(1, 2 * NY):
        pltpu.make_async_copy(votes.at[mom], votes.at[mom], send_vote.at[step]).wait()


def per_device(peramb, elementals, pair_times, pair_order, class_group, gamma_columns, gamma_phases):
    smem = pl.BlockSpec(memory_space=pltpu.SMEM)
    anywhere = pl.BlockSpec(memory_space=pl.ANY)
    dma = pltpu.SemaphoreType.DMA
    found = pl.pallas_call(
        correlator_kernel,
        out_shape=jax.ShapeDtypeStruct((8, 128), F32),
        in_specs=[smem] * 5 + [anywhere] * 2,
        out_specs=pl.BlockSpec(memory_space=pltpu.VMEM),
        scratch_shapes=[
            pltpu.VMEM((NX * NZ, ROWS, PIECE), BF16),
            pltpu.VMEM((NX * NZ, ROWS, PIECE), BF16),
            pltpu.VMEM((2, PEERS, ROWS, PIECE), BF16),
            pltpu.VMEM((NY, 2, PEERS, ROWS, PIECE), BF16),
            pltpu.VMEM(elementals.shape, BF16),
            pltpu.VMEM((FULL, 2 * FULL), BF16),
            pltpu.VMEM((SPINS, 2, FULL, 256), BF16),
            pltpu.VMEM((SPINS, 2, FULL, 256), BF16),
            pltpu.VMEM((2, SPINS, VECTORS, 3 * FULL), BF16),
            pltpu.VMEM((2, SPINS, VECTORS, 3 * FULL), BF16),
            pltpu.VMEM((2, FULL, FULL), F32),
            pltpu.VMEM((2, FULL, FULL), F32),
            pltpu.VMEM((2 * NY, 8, 128), F32),
            dma((3,)),
            dma((2,)),
            dma((2,)),
            dma((2, STEPS)),
            dma((2, STEPS)),
            dma((2, STEPS)),
            dma((4, STEPS)),
            dma((4, STEPS)),
            dma((2 * NY,)),
            dma((2 * NY,)),
        ],
        compiler_params=pltpu.CompilerParams(
            collective_id=0, has_side_effects=True, vmem_limit_bytes=60 * 1024 * 1024
        ),
        cost_estimate=pl.CostEstimate(flops=11_000_000_000, bytes_accessed=8_000_000, transcendentals=0),
        name="correlator",
    )(pair_order, pair_times.T, gamma_columns, gamma_phases, class_group, peramb, elementals)
    return found[:2, :GROUPS].reshape(2, 1, GROUPS)


def solution(mesh):
    placed = (P(None, "pair", None), P(None, "mom", None, None, None), P(), P(), P("mom"), P(), P())
    return jax.shard_map(
        per_device, mesh=mesh, in_specs=placed, out_specs=P(None, "pair", None), check_vma=False
    )
```
